128 devices in a mesh: gx: 8 (over y, core), gy: 16 (over x, z).
Axes of the slice: x: 4, y: 4, z: 4, core: 2. Of those that a mesh axis runs over, the one named last changes fastest.
Arguments:
- a_blocks: bfloat16 [3072, 7, 256, 256], P(('gx', 'gy'))
- prolong: bfloat16 [3072, 256, 128], P(('gx', 'gy'))
- neighbour: int32 [3072, 6], P(('gx', 'gy')), may hold values from 0 to 71, as said below
- ghost_send: int32 [8, 16, 16, 3], P('gx', 'gy'), may hold values from 0 to 23
- fine_agg: int32 [3072], P(('gx', 'gy')), may hold values from 0 to 255, as said below
- balance: int32 [8, 16, 16], P('gx', 'gy'), may hold values from 0 to 128, as said below
- coarse_cols: int32 [1024, 7], P(('gx', 'gy')), may hold values from 0 to 1023, as said below
- loads: bfloat16 [1024, 128, 256], P(('gx', 'gy')), may hold values from -48 to 48
Outputs:
- coarse: bfloat16 [1024, 7, 128, 128], P(('gx', 'gy'))
- smoothed: bfloat16 [1024, 128, 256], P(('gx', 'gy'))
The draws below stay inside these ranges and needn't reach their ends.
Inputs may be any that keep to these rules, and one draw needn't show every extreme that they name: `neighbour`: an entry below 24 names a block row of the same device. An entry v >= 24 names slot (v - 24) % 3 of the blocks sent by the device of the same gx row at gy index (v - 24) // 3, never the device itself; every slot so named is named at least once, and the slots named from one peer are the first few of its 3; some device names all 3 slots of some peer. `fine_agg`: the owner is a device of the same gx row. Each aggregate is named by exactly three fine block rows, on three different devices. At most 3 block rows of one device name aggregates of one owner, and this is reached in every draw. Every named slot has a balance entry below 128, and some owner holds 16 aggregates. `balance`: entry 128 marks a slot that no block row names. Every coarse row of a gx row receives exactly one slot, and one owner sends at most one aggregate to each device. At most 3 block rows of one device have their target coarse row on one device, and this is reached in every draw. coarse_cols[g, 0] = g; the other entries name coarse rows of the same device or of a device whose gy index differs by one, in the same gx row.
All inputs are finite; a program needn't handle non-finite values.
Results may differ from the reference program's by a relative error of at most 0.0051.
Values may be sent and summed in bfloat16 or wider, within the bound.
A program may use at most 128 MiB of HBM per device.

```python
import math
import jax
import jax.numpy as jnp
from jax import lax

BS = 256
CB = 128
LOADS = 256
K = 7
GCAP = 3
SWEEPS = 2
RB = 24
CR = 8
NF = 3072
NCR = 1024
N_GX = 8
N_GY = 16
DEVICES = 128


def ownership(key):
    total = N_GY * CR
    if N_GY % 3 == 1:
        inverse_three = (2 * N_GY + 1) // 3
    else:
        inverse_three = (N_GY + 1) // 3
    first_count = min(3, CR)

    def one_row(row_key):
        sub_keys = jax.random.split(row_key, 6)
        q_index = jnp.arange(total, dtype=jnp.int32)
        grid_row = q_index // N_GY
        grid_col = q_index % N_GY
        hot_row = jax.random.randint(sub_keys[0], (), 0, CR).astype(jnp.int32)
        valid = (grid_col > 0) & (grid_row != hot_row)
        scores = jax.random.permutation(sub_keys[1], total).astype(jnp.int32)
        scores = jnp.where(valid, scores, -1)
        order = jnp.argsort(-scores, stable=True).astype(jnp.int32)
        rank = jnp.zeros((total,), jnp.int32).at[order].set(q_index)
        cut_inner = valid & (rank < N_GY - CR)
        start_flag = (grid_col == 0) | cut_inner
        segment = (jnp.cumsum(start_flag.astype(jnp.int32)) - 1).astype(jnp.int32)
        segment_start = lax.cummax(jnp.where(start_flag, q_index, 0), axis=0)
        slot_of = (q_index - segment_start).astype(jnp.int32)
        owner_label = jax.random.permutation(sub_keys[2], N_GY).astype(jnp.int32)[segment]
        base = jax.random.randint(sub_keys[3], (), 0, N_GY).astype(jnp.int32)
        first_offsets = (base - inverse_three * jnp.arange(first_count, dtype=jnp.int32)) % N_GY
        shuffled = jax.random.permutation(sub_keys[4], N_GY).astype(jnp.int32)
        taken = jnp.any(shuffled[:, None] == first_offsets[None, :], axis=1).astype(jnp.int32)
        remaining = shuffled[jnp.argsort(taken, stable=True)]
        offsets = jnp.concatenate([first_offsets, remaining[:CR - first_count]]).astype(jnp.int32)
        receiver = ((grid_col + offsets[grid_row]) % N_GY).astype(jnp.int32)
        order_keys = jax.random.split(sub_keys[5], N_GY)
        orders = jax.vmap(lambda one_key: jax.random.permutation(one_key, CR).astype(jnp.int32))(order_keys)
        coarse_index = (receiver * CR + orders[receiver, grid_row]).astype(jnp.int32)
        position = jnp.arange(N_GY * RB, dtype=jnp.int32)
        q_of_position = position // 3
        values = owner_label[q_of_position] * N_GY + slot_of[q_of_position]
        fine_values = values.reshape(RB, N_GY).T
        slot_table = jnp.full((N_GY, N_GY), N_GY * CR, jnp.int32).at[owner_label, slot_of].set(coarse_index)
        return (fine_values.reshape(-1).astype(jnp.int32), slot_table)
    row_keys = jax.random.split(key, N_GX)
    return jax.vmap(one_row)(row_keys)


def draw_fine_agg(key, part):
    fine_values, tables = ownership(jax.random.fold_in(key, 11))
    return fine_values.reshape(-1).astype(jnp.int32)


def draw_balance(key, part):
    fine_values, tables = ownership(jax.random.fold_in(key, 11))
    return tables.astype(jnp.int32)


def draw_neighbour(key, part):
    entries = RB * (K - 1)

    def one_device(device_key, device):
        sub_keys = jax.random.split(device_key, 4)
        self_gy = device % N_GY
        counts = jax.random.randint(sub_keys[0], (N_GY,), 0, GCAP).astype(jnp.int32)
        shuffled = jax.random.permutation(sub_keys[1], N_GY).astype(jnp.int32)
        moved = jnp.argsort((shuffled == self_gy).astype(jnp.int32))
        first_peer = shuffled[moved[0]]
        second_peer = shuffled[moved[1]]
        counts = counts.at[first_peer].set(GCAP).at[second_peer].set(GCAP).at[self_gy].set(0)
        live_slot = (jnp.arange(GCAP, dtype=jnp.int32)[None, :] < counts[:, None]).reshape(-1)
        live_rank = jnp.cumsum(live_slot.astype(jnp.int32)) - 1
        positions = jax.random.permutation(sub_keys[2], entries).astype(jnp.int32)
        values = jax.random.randint(sub_keys[3], (entries,), 0, RB).astype(jnp.int32)
        slot_value = RB + jnp.arange(N_GY * GCAP, dtype=jnp.int32)
        where_to = jnp.where(live_slot, positions[jnp.clip(live_rank, 0, entries - 1)], entries)
        values = values.at[where_to].set(slot_value, mode='drop')
        return values.reshape(RB, K - 1)
    device_keys = jax.random.split(key, DEVICES)
    result = jax.vmap(one_device)(device_keys, jnp.arange(DEVICES, dtype=jnp.int32))
    return result.reshape(NF, K - 1)


def draw_coarse_cols(key, part):
    rows_all = DEVICES * CR
    row_ids = jnp.arange(rows_all, dtype=jnp.int32)
    device = row_ids // CR
    gy_pos = device % N_GY
    sub_keys = jax.random.split(key, 2)
    device_step = jax.random.randint(sub_keys[0], (rows_all, K - 1), -1, 2).astype(jnp.int32)
    near_gy = jnp.clip(gy_pos[:, None] + device_step, 0, N_GY - 1)
    chosen = jax.random.randint(sub_keys[1], (rows_all, K - 1), 0, CR).astype(jnp.int32)
    others = (device[:, None] - gy_pos[:, None] + near_gy) * CR + chosen
    return jnp.concatenate([row_ids[:, None], others], axis=1).astype(jnp.int32)


def draw_a_blocks(key, part):
    coherent = jnp.where(jnp.arange(K) == 0, 2.0, -1.0 / 3.0).astype(jnp.float32)[:, None, None] * jnp.eye(BS, dtype=jnp.float32)[None]
    noise_scale = 1.0 / math.sqrt(BS)

    def one_row(row_index):
        row_key = jax.random.fold_in(key, row_index)
        sub_keys = jax.random.split(row_key, 2)
        noise_part = jax.random.normal(sub_keys[0], (K, BS, BS), jnp.float32)
        spread = jnp.exp(jax.random.uniform(sub_keys[1], (), jnp.float32, 0.0, math.log(10.0)))
        rise_factor = 1.0 + 2.0 * row_index.astype(jnp.float32) / (NF - 1)
        row_scale = spread * rise_factor / 32.0
        return ((coherent + noise_part * noise_scale) * row_scale).astype(jnp.bfloat16)
    return lax.map(one_row, jnp.arange(NF, dtype=jnp.int32))


def draw_prolong(key, part):
    noise_part = jax.random.normal(key, (NF, BS, CB), jnp.float32)
    identity = jnp.eye(BS, CB, dtype=jnp.float32)
    return (noise_part / math.sqrt(BS) + identity[None]).astype(jnp.bfloat16)


def set_ends(drawn, stream_key, least, high):
    place = [jax.random.randint(jax.random.fold_in(stream_key, axis), (), 0, length) for axis, length in enumerate(drawn.shape)]
    main_axis = drawn.shape.index(max(drawn.shape))
    beside = place[:main_axis] + [(place[main_axis] + 1) % drawn.shape[main_axis]] + place[main_axis + 1:]
    return drawn.at[tuple(place)].set(least).at[tuple(beside)].set(high)


def steps_of(stream_key, dims, shards, least, high):
    gain, own = 1.0, jax.random.fold_in(stream_key, 6)
    for dim, shards_of in shards:
        draws = jnp.exp(jax.random.uniform(jax.random.fold_in(own, dim), (shards_of,), jnp.float32, least / len(shards), high / len(shards)))
        gain = gain * jnp.repeat(draws, dims[dim] // shards_of).reshape([-1 if axis == dim else 1 for axis in range(len(dims))])
    return gain


def gaussian(stream_key, shape, width, most, shards=(), held_as=jnp.bfloat16):
    array = jax.random.normal(stream_key, shape, jnp.float32) * width
    if len(shards) > 0:
        array = steps_of(stream_key, shape, shards, -0.22, 0.18) * array
    return jnp.clip(array, min=-most, max=most).astype(held_as)


def setup_inputs(seed: int = 0) -> dict:
    key_of = jax.random.split(jax.random.key(seed), 9)
    return {
        "a_blocks": draw_a_blocks(jax.random.fold_in(key_of[8], 71), 0),
        "prolong": draw_prolong(jax.random.fold_in(key_of[8], 71), 0),
        "neighbour": draw_neighbour(jax.random.fold_in(key_of[8], 71), 0),
        "ghost_send": set_ends(jax.random.randint(key_of[3], (N_GX, N_GY, N_GY, GCAP), 0, RB), jax.random.fold_in(key_of[3], 1), 0, RB - 1).astype(jnp.int32),
        "fine_agg": draw_fine_agg(jax.random.fold_in(key_of[8], 71), 0),
        "balance": draw_balance(jax.random.fold_in(key_of[8], 71), 0),
        "coarse_cols": draw_coarse_cols(jax.random.fold_in(key_of[8], 71), 0),
        "loads": gaussian(key_of[7], (NCR, CB, LOADS), 8.0, 48.0, ((0, 128),)),
    }


def reference(a_blocks, prolong, neighbour, ghost_send, fine_agg, balance, coarse_cols, loads):
    group_size = N_GY
    total_rows = a_blocks.shape[0]
    device_of = jnp.arange(total_rows, dtype=jnp.int32) // RB
    gx_of = device_of // group_size
    gy_of = device_of % group_size
    remote = neighbour - RB
    peer_index = jnp.clip(remote // GCAP, 0, group_size - 1).astype(jnp.int32)
    cap_index = jnp.clip(remote % GCAP, 0, GCAP - 1).astype(jnp.int32)
    sent_block = ghost_send[gx_of[:, None], peer_index, gy_of[:, None], cap_index]
    remote_row = (gx_of[:, None] * group_size + peer_index) * RB + sent_block
    local_row = device_of[:, None] * RB + neighbour
    column_rows = jnp.where(neighbour < RB, local_row, remote_row).astype(jnp.int32)
    columns = jnp.concatenate([jnp.arange(total_rows, dtype=jnp.int32)[:, None], column_rows], axis=1)

    def one_row(row_inputs):
        blocks, left_block, column_ids = row_inputs
        right_blocks = prolong[column_ids]
        applied = jnp.einsum("kab,kbc->kac", blocks.astype(jnp.float32), right_blocks.astype(jnp.float32),
                             precision=lax.Precision.HIGHEST).astype(jnp.bfloat16)
        return jnp.einsum("ac,kad->kcd", left_block.astype(jnp.float32), applied.astype(jnp.float32),
                          precision=lax.Precision.HIGHEST).astype(jnp.bfloat16)

    partial_value = lax.map(one_row, (a_blocks, prolong, columns))
    slot_count = balance.shape[2]
    flat_balance = balance.reshape(-1)
    key_index = gx_of * (group_size * slot_count) + fine_agg
    target = (gx_of * (group_size * CR) + flat_balance[key_index]).astype(jnp.int32)
    coarse_rows = loads.shape[0]
    summed = jax.ops.segment_sum(partial_value.astype(jnp.float32), target, num_segments=coarse_rows)
    coarse = summed.astype(jnp.bfloat16)

    magnitude = jnp.sum(jnp.abs(coarse.astype(jnp.float32)), axis=(1, 3))
    largest = jnp.max(magnitude)
    lower_end = largest / 30.0
    centre = (largest + lower_end) / 2.0
    half_width = (largest - lower_end) / 2.0
    sigma_ratio = centre / half_width
    right_side = loads.astype(jnp.float32)
    solution = right_side / centre
    update = solution
    weight_now = 1.0 / sigma_ratio
    for sweep_index in range(SWEEPS):
        rounded = solution.astype(jnp.bfloat16)
        accumulated = jnp.zeros(right_side.shape, jnp.float32)
        for column_slot in range(K):
            picked = rounded[coarse_cols[:, column_slot]]
            accumulated = accumulated + jnp.einsum(
                "gab,gbl->gal", coarse[:, column_slot].astype(jnp.float32), picked.astype(jnp.float32),
                precision=lax.Precision.HIGHEST)
        residual = right_side - accumulated
        weight_next = 1.0 / (2.0 * sigma_ratio - weight_now)
        update = weight_next * weight_now * update + (2.0 * weight_next / half_width) * residual
        solution = solution + update
        weight_now = weight_next
    return coarse, solution.astype(jnp.bfloat16)
```

```python
import functools

import jax
import jax.numpy as jnp
from jax import lax
from jax.experimental import pallas as pl
from jax.experimental.pallas import tpu as pltpu
from jax.sharding import PartitionSpec as P

MESH = pl.DeviceIdType.MESH
NX = 4
NZ = 4
GCAP = 3
LINE = 12
SWEEPS = 2
CHUNKS = ((0, 3), (3, 6), (6, 7))
VMEM = pltpu.VMEM
SMEM = pltpu.SMEM
DMA = pltpu.SemaphoreType.DMA


def place():
    me = lax.axis_index("gy")
    return lax.axis_index("gx"), lax.div(me, NZ), lax.rem(me, NZ)


def line_peer(axis, step):
    gx, x, z = place()
    if axis == 0:
        return gx, lax.rem(x + step, NX) * NZ + z
    return gx, x * NZ + lax.rem(z + step, NZ)


def greet(peers):
    barrier = pltpu.get_barrier_semaphore()
    for peer in peers:
        pl.semaphore_signal(barrier, 1, device_id=peer, device_id_type=MESH)
    pl.semaphore_wait(barrier, len(peers))


def remote(src, dst, send, recv, peer):
    return pltpu.make_async_remote_copy(
        src_ref=src, dst_ref=dst, send_sem=send, recv_sem=recv, device_id=peer, device_id_type=MESH
    )


def ghost_kernel(
    prolong, sends, table, ghosts, tables, packed, held, own_sem,
    send1, recv1, send2, recv2, tsend1, trecv1, tsend2, trecv2, keep_sem, tkeep,
):
    gx, x, z = place()
    coords = (x, z)
    half = prolong.shape[1] // 2
    greet([line_peer(axis, step) for axis in (0, 1) for step in (1, 2, 3)])

    own_table = pltpu.make_async_copy(table, tables.at[x, z], tkeep.at[0])
    own_table.start()
    first = []
    for step in (1, 2, 3):
        copy = remote(table, tables.at[x, z], tsend1.at[step - 1], trecv1.at[step - 1], line_peer(0, step))
        copy.start()
        first.append(copy)

    started = []
    for step in (1, 2, 3, 0):
        for axis in (0, 1):
            near = lax.rem(coords[axis] + step, 4)

            def pack(n, carry, axis=axis, step=step, near=near):
                far, c = lax.div(n, GCAP), lax.rem(n, GCAP)
                peer = near * NZ + far if axis == 0 else far * NZ + near
                packed[axis, step, n] = prolong[sends[peer, c], axis * half : (axis + 1) * half, :]
                return carry

            lax.fori_loop(0, 4 * GCAP, pack, 0)
            if step:
                copy = remote(
                    packed.at[axis, step], held.at[axis, step - 1],
                    send1.at[axis, step - 1], recv1.at[axis, step - 1], line_peer(axis, step),
                )
                copy.start()
                started.append(copy)

    def rows(axis, px, pz):
        first_row = (px * NZ + pz) * GCAP
        return ghosts.at[pl.ds(first_row, GCAP), pl.ds(axis * half, half), :]

    def source_of(axis, back):
        near = lax.rem(coords[axis] + 4 - back, 4)
        return (near, z) if axis == 0 else (x, near)

    second = []
    kept = []
    for back in (0, 1, 2, 3):
        for axis in (0, 1):
            if back:
                remote(
                    packed.at[axis, back], held.at[axis, back - 1],
                    send1.at[axis, back - 1], recv1.at[axis, back - 1], line_peer(axis, back),
                ).wait_recv()
            at = packed.at[axis, 0] if back == 0 else held.at[axis, back - 1]
            px, pz = source_of(axis, back)
            for step in (1, 2, 3):
                far = lax.rem(coords[1 - axis] + step, 4)
                copy = remote(
                    at.at[pl.ds(far * GCAP, GCAP)], rows(axis, px, pz),
                    send2.at[axis, back, step - 1], recv2.at[axis, back, step - 1], line_peer(1 - axis, step),
                )
                copy.start()
                second.append(copy)
            copy = pltpu.make_async_copy(
                at.at[pl.ds(coords[1 - axis] * GCAP, GCAP)], rows(axis, px, pz), keep_sem.at[axis, back]
            )
            copy.start()
            kept.append(copy)
        if back == 0:
            own_table.wait()
        else:
            first[back - 1].wait_recv()
        px = lax.rem(x + 4 - back, 4)
        for step in (1, 2, 3):
            copy = remote(
                tables.at[px, z], tables.at[px, z],
                tsend2.at[back, step - 1], trecv2.at[back, step - 1], line_peer(1, step),
            )
            copy.start()
            second.append(copy)
    for copy in kept:
        copy.wait()
    for copy in started + first:
        copy.wait_send()
    for copy in second:
        copy.wait_send()
    for back in (0, 1, 2, 3):
        px = lax.rem(x + 4 - back, 4)
        for step in (1, 2, 3):
            pz = lax.rem(z + 4 - step, 4)
            remote(
                tables.at[px, pz], tables.at[px, pz],
                tsend2.at[back, step - 1], trecv2.at[back, step - 1], line_peer(1, step),
            ).wait_recv()
            for axis in (0, 1):
                near = lax.rem(coords[axis] + 4 - back, 4)
                far = lax.rem(coords[1 - axis] + 4 - step, 4)
                place_of = rows(axis, near, far) if axis == 0 else rows(axis, far, near)
                remote(
                    place_of, place_of,
                    send2.at[axis, back, step - 1], recv2.at[axis, back, step - 1], line_peer(1 - axis, step),
                ).wait_recv()


def exchange_ghosts(prolong, sends, table):
    rows, order, width = prolong.shape
    peers = NX * NZ
    return pl.pallas_call(
        ghost_kernel,
        out_shape=(
            jax.ShapeDtypeStruct((peers * GCAP, order, width), prolong.dtype),
            jax.ShapeDtypeStruct((NX, NZ, 8, 128), jnp.int32),
        ),
        in_specs=[
            pl.BlockSpec(memory_space=VMEM),
            pl.BlockSpec(memory_space=SMEM),
            pl.BlockSpec(memory_space=VMEM),
        ],
        out_specs=(pl.BlockSpec(memory_space=pl.ANY), pl.BlockSpec(memory_space=VMEM)),
        scratch_shapes=[
            VMEM((2, 4, 4 * GCAP, order // 2, width), prolong.dtype),
            VMEM((2, 3, 4 * GCAP, order // 2, width), prolong.dtype),
            DMA((1,)),
            DMA((2, 3)), DMA((2, 3)), DMA((2, 4, 3)), DMA((2, 4, 3)),
            DMA((3,)), DMA((3,)), DMA((4, 3)), DMA((4, 3)),
            DMA((2, 4)), DMA((1,)),
        ],
        compiler_params=pltpu.CompilerParams(
            collective_id=1, has_side_effects=True, vmem_limit_bytes=24 << 20
        ),
    )(prolong, sends, table)


def table_kernel(slots, coarse_rows, tables, packs, merges, count, number):
    gx, x, z = place()
    fine_rows = 24
    for half in (0, 1):
        def clear_merge(n, carry, half=half):
            merges[half, n] = 4 * LINE
            return carry

        def clear_pack(n, carry, half=half):
            packs[half, n] = 0
            return carry

        def clear_number(n, carry):
            number[n] = 0
            return carry

        lax.fori_loop(0, 4 * coarse_rows * 3, clear_merge, 0)
        lax.fori_loop(0, 4 * LINE, clear_pack, 0)
        lax.fori_loop(0, 4 * coarse_rows, clear_number, 0)
        mine = x if half == 0 else z

        def from_source(s, carry, half=half, mine=mine):
            dx, dz = (s, z) if half == 0 else (x, s)
            for n in range(4):
                count[n] = 0

            def one_row(i, inner):
                label = tables[dx, dz, 0, i]
                owner, slot = lax.div(label, slots), lax.rem(label, slots)
                target = tables[lax.div(owner, NZ), lax.rem(owner, NZ), 1, slot]
                device, row = lax.div(target, coarse_rows), lax.rem(target, coarse_rows)
                tx, tz = lax.div(device, NZ), lax.rem(device, NZ)
                near, far = (tx, tz) if half == 0 else (tz, tx)
                rank = count[near]
                count[near] = rank + 1

                @pl.when(near == mine)
                def _():
                    goal = far * coarse_rows + row
                    done = number[goal]
                    merges[half, goal * 3 + done] = s * LINE + rank
                    number[goal] = done + 1

                @pl.when(s == mine)
                def _():
                    packs[half, near * LINE + rank] = i

                return inner

            lax.fori_loop(0, fine_rows, one_row, 0)
            return carry

        lax.fori_loop(0, 4, from_source, 0)


def make_tables(tables, slots, coarse_rows):
    return pl.pallas_call(
        functools.partial(table_kernel, slots, coarse_rows),
        out_shape=(
            jax.ShapeDtypeStruct((2, 4 * LINE), jnp.int32),
            jax.ShapeDtypeStruct((2, 4 * coarse_rows * 3), jnp.int32),
        ),
        in_specs=[pl.BlockSpec(memory_space=SMEM)],
        out_specs=(pl.BlockSpec(memory_space=SMEM), pl.BlockSpec(memory_space=SMEM)),
        scratch_shapes=[SMEM((4,), jnp.int32), SMEM((4 * coarse_rows,), jnp.int32)],
    )(tables)


def product_kernel(neighbour, blocks, prolong, ghosts, partial, pool, applied, sems):
    i = pl.program_id(0)
    rows = prolong.shape[0]
    pieces, width = blocks.shape[1], prolong.shape[2]

    @pl.when(i == 0)
    def _():
        copies = [
            pltpu.make_async_copy(prolong, pool.at[pl.ds(0, rows)], sems.at[0]),
            pltpu.make_async_copy(ghosts, pool.at[pl.ds(rows, ghosts.shape[0])], sems.at[1]),
        ]
        for copy in copies:
            copy.start()
        for copy in copies:
            copy.wait()

    for k in range(pieces):
        column = i if k == 0 else neighbour[i, k - 1]
        applied[:, k * width : (k + 1) * width] = jnp.dot(
            blocks[0, k], pool[column], preferred_element_type=jnp.float32
        ).astype(applied.dtype)
    left = pool[i]
    result = lax.dot_general(
        left, applied[...], (((0,), (0,)), ((), ())), preferred_element_type=jnp.float32
    ).astype(partial.dtype)
    for k in range(pieces):
        partial[0, k] = result[:, k * width : (k + 1) * width]


def products(a_blocks, prolong, ghosts, neighbour):
    rows, pieces, order, _ = a_blocks.shape
    width = prolong.shape[2]
    pool = rows + ghosts.shape[0]
    return pl.pallas_call(
        product_kernel,
        grid_spec=pltpu.PrefetchScalarGridSpec(
            num_scalar_prefetch=1,
            grid=(rows,),
            in_specs=[
                pl.BlockSpec((1, pieces, order, order), lambda i, n: (i, 0, 0, 0)),
                pl.BlockSpec(memory_space=pl.ANY),
                pl.BlockSpec(memory_space=pl.ANY),
            ],
            out_specs=pl.BlockSpec((1, pieces, width, width), lambda i, n: (i, 0, 0, 0)),
            scratch_shapes=[
                VMEM((pool, order, width), prolong.dtype),
                VMEM((order, pieces * width), prolong.dtype),
                DMA((2,)),
            ],
        ),
        out_shape=jax.ShapeDtypeStruct((rows, pieces, width, width), prolong.dtype),
        compiler_params=pltpu.CompilerParams(
            dimension_semantics=("arbitrary",), vmem_limit_bytes=32 << 20
        ),
        cost_estimate=pl.CostEstimate(
            flops=2 * rows * pieces * order * width * (order + width),
            bytes_accessed=2 * rows * pieces * order * order,
            transcendentals=0,
        ),
    )(neighbour, a_blocks, prolong, ghosts)


def coarse_kernel(
    n_gx, partial, packs, merges, cols, loads, coarse, smoothed,
    low, high, pad0, pad1, state, change, peak, peaks,
    send1, recv1, send2, recv2, hsend, hrecv, psend, precv, *bufs,
):
    gx, x, z = place()
    gy = x * NZ + z
    coords = (x, z)
    count = NX * NZ
    width = partial.shape[2]
    half = width // 2
    rows = loads.shape[0]
    n_chunks = len(CHUNKS)
    out, pool, sums, back = (bufs[2 * n_chunks * n : 2 * n_chunks * (n + 1)] for n in range(4))
    up = (gx, lax.rem(gy + 1, count))
    down = (gx, lax.rem(gy + count - 1, count))
    across = [(lax.rem(gx + step, n_gx), gy) for step in range(1, n_gx)]
    lines = [line_peer(axis, step) for axis in (0, 1) for step in (1, 2, 3)]
    greet(lines + [up, down] + across)

    first = []
    for c, (k0, k1) in enumerate(CHUNKS):
        for step in (1, 2, 3, 0):
            for axis in (0, 1):
                b = 2 * c + axis
                near = lax.rem(coords[axis] + step, 4)

                def pack(n, carry, axis=axis, step=step, near=near, b=b, k0=k0, k1=k1):
                    value = partial[packs[axis, near * LINE + n], k0:k1, axis * half : (axis + 1) * half, :]
                    if step:
                        out[b][step - 1, n] = value
                    else:
                        pool[b][near * LINE + n] = value
                    return carry

                lax.fori_loop(0, LINE, pack, 0)
                if step:
                    copy = remote(
                        out[b].at[step - 1], pool[b].at[pl.ds(coords[axis] * LINE, LINE)],
                        send1.at[b, step - 1], recv1.at[b, step - 1], line_peer(axis, step),
                    )
                    copy.start()
                    first.append(copy)
                else:
                    pool[b][4 * LINE] = jnp.zeros(pool[b].shape[1:], pool[b].dtype)

    second = []
    for c, (k0, k1) in enumerate(CHUNKS):
        for axis in (0, 1):
            b = 2 * c + axis
            for step in (1, 2, 3):
                source = lax.rem(coords[axis] + 4 - step, 4)
                remote(
                    out[b].at[step - 1], pool[b].at[pl.ds(source * LINE, LINE)],
                    send1.at[b, step - 1], recv1.at[b, step - 1], line_peer(axis, step),
                ).wait_recv()
            for step in (1, 2, 3, 0):
                far = lax.rem(coords[1 - axis] + step, 4)

                def merge(r, carry, axis=axis, b=b, step=step, far=far, k0=k0, k1=k1):
                    at = (far * rows + r) * 3
                    terms = [merges[axis, at + n] for n in range(3)]
                    for k in range(k1 - k0):
                        total = pool[b][terms[0], k].astype(jnp.float32)
                        total += pool[b][terms[1], k].astype(jnp.float32)
                        total += pool[b][terms[2], k].astype(jnp.float32)
                        sums[b][step, r, k] = total.astype(jnp.bfloat16)
                    return carry

                lax.fori_loop(0, rows, merge, 0)
                if step:
                    copy = remote(
                        sums[b].at[step], back[b].at[step - 1],
                        send2.at[b, step - 1], recv2.at[b, step - 1], line_peer(1 - axis, step),
                    )
                    copy.start()
                    second.append(copy)

    halo = [
        remote(loads, low, hsend.at[0], hrecv.at[0], up),
        remote(loads, high, hsend.at[1], hrecv.at[1], down),
    ]
    for copy in halo:
        copy.start()

    for n, (c, (k0, k1)) in enumerate(list(enumerate(CHUNKS))):
        for axis in (0, 1):
            b = 2 * c + axis
            for step in (1, 2, 3):
                second[6 * c + 3 * axis + step - 1].wait_recv()

            def finish(r, carry, axis=axis, b=b, k0=k0, k1=k1):
                for k in range(k1 - k0):
                    total = sums[b][0, r, k].astype(jnp.float32)
                    for step in (1, 2, 3):
                        total += back[b][step - 1, r, k].astype(jnp.float32)
                    coarse[r, k0 + k, axis * half : (axis + 1) * half, :] = total.astype(jnp.bfloat16)
                return carry

            lax.fori_loop(0, rows, finish, 0)

    peak[...] = jnp.zeros(peak.shape, peak.dtype)

    def row_peak(r, carry):
        total = jnp.zeros((width, width), jnp.float32)
        for k in range(coarse.shape[1]):
            total += jnp.abs(coarse[r, k].astype(jnp.float32))
        top = jnp.max(jnp.sum(total, axis=1, keepdims=True), axis=0, keepdims=True)
        peak[0] = jnp.maximum(peak[0], jnp.broadcast_to(top, peak.shape[1:]))
        return carry

    lax.fori_loop(0, rows, row_peak, 0)

    base = 0
    for stage, peers in enumerate((lines[:3], lines[3:], across)):
        copies = []
        for n, peer in enumerate(peers):
            copy = remote(peak.at[stage], peaks.at[base + n], psend.at[base + n], precv.at[base + n], peer)
            copy.start()
            copies.append(copy)
        for copy in copies:
            copy.wait()
        top = peak[stage]
        for n in range(len(peers)):
            top = jnp.maximum(top, peaks[base + n])
        peak[stage + 1] = top
        base += len(peers)

    largest = peak[3, 0:1, 0:1]
    lower_end = largest / 30.0
    centre = (largest + lower_end) / 2.0
    half_width = (largest - lower_end) / 2.0
    sigma = centre / half_width
    weight = 1.0 / sigma

    def begin(r, carry):
        value = loads[r].astype(jnp.float32) / centre
        state[r] = value
        change[r] = value
        pad0[rows + r] = value.astype(jnp.bfloat16)
        return carry

    lax.fori_loop(0, rows, begin, 0)
    for copy in halo:
        copy.wait()

    def sides(r, carry):
        pad0[r] = (low[r].astype(jnp.float32) / centre).astype(jnp.bfloat16)
        pad0[2 * rows + r] = (high[r].astype(jnp.float32) / centre).astype(jnp.bfloat16)
        return carry

    lax.fori_loop(0, rows, sides, 0)

    for sweep in range(SWEEPS):
        pad = (pad0, pad1)[sweep]
        following = 1.0 / (2.0 * sigma - weight)
        keep = following * weight
        gain = 2.0 * following / half_width

        def row(r, carry, pad=pad, keep=keep, gain=gain, sweep=sweep):
            product = jnp.zeros(state.shape[1:], jnp.float32)
            for k in range(coarse.shape[1]):
                product += jnp.dot(
                    coarse[r, k], pad[cols[r, k]], preferred_element_type=jnp.float32
                )
            residual = loads[r].astype(jnp.float32) - product
            update = keep * change[r] + gain * residual
            value = state[r] + update
            if sweep + 1 < SWEEPS:
                change[r] = update
                state[r] = value
                pad1[rows + r] = value.astype(jnp.bfloat16)
            else:
                smoothed[r] = value.astype(jnp.bfloat16)
            return carry

        lax.fori_loop(0, rows, row, 0)
        weight = following
        if sweep + 1 < SWEEPS:
            own = pad1.at[pl.ds(rows, rows)]
            copies = [
                remote(own, pad1.at[pl.ds(0, rows)], hsend.at[2], hrecv.at[2], up),
                remote(own, pad1.at[pl.ds(2 * rows, rows)], hsend.at[3], hrecv.at[3], down),
            ]
            for copy in copies:
                copy.start()
            for copy in copies:
                copy.wait()
    for copy in first + second:
        copy.wait_send()


def coarse_and_smooth(n_gx, partial, packs, merges, cols, loads):
    _, pieces, width, _ = partial.shape
    rows, _, columns = loads.shape
    half = width // 2
    bf16, f32 = jnp.bfloat16, jnp.float32
    n_b = 2 * len(CHUNKS)
    peers = 6 + n_gx - 1
    spans = [k1 - k0 for k0, k1 in CHUNKS for _ in range(2)]
    bufs = [VMEM((3, LINE, n, half, width), bf16) for n in spans]
    bufs += [VMEM((4 * LINE + 1, n, half, width), bf16) for n in spans]
    bufs += [VMEM((4, rows, n, half, width), bf16) for n in spans]
    bufs += [VMEM((3, rows, n, half, width), bf16) for n in spans]
    vmem, smem = pl.BlockSpec(memory_space=VMEM), pl.BlockSpec(memory_space=SMEM)
    return pl.pallas_call(
        functools.partial(coarse_kernel, n_gx),
        out_shape=(
            jax.ShapeDtypeStruct((rows, pieces, width, width), bf16),
            jax.ShapeDtypeStruct((rows, width, columns), bf16),
        ),
        in_specs=[vmem, smem, smem, smem, vmem],
        out_specs=(vmem, vmem),
        scratch_shapes=[
            VMEM((rows, width, columns), bf16),
            VMEM((rows, width, columns), bf16),
            VMEM((3 * rows, width, columns), bf16),
            VMEM((3 * rows, width, columns), bf16),
            VMEM((rows, width, columns), f32),
            VMEM((rows, width, columns), f32),
            VMEM((4, 8, 128), f32),
            VMEM((peers, 8, 128), f32),
            DMA((n_b, 3)), DMA((n_b, 3)), DMA((n_b, 3)), DMA((n_b, 3)),
            DMA((4,)), DMA((4,)), DMA((peers,)), DMA((peers,)),
            *bufs,
        ],
        compiler_params=pltpu.CompilerParams(
            collective_id=2, has_side_effects=True, vmem_limit_bytes=58 << 20
        ),
    )(partial, packs, merges, cols, loads)


def per_device(n_gx, a_blocks, prolong, neighbour, ghost_send, fine_agg, balance, coarse_cols, loads):
    slots = balance.shape[2]
    table = jnp.concatenate(
        [
            jnp.pad(fine_agg, (0, 128 - fine_agg.shape[0]))[None],
            jnp.pad(balance[0, 0], (0, 128 - slots))[None],
            jnp.zeros((6, 128), jnp.int32),
        ]
    )
    ghosts, tables = exchange_ghosts(prolong, ghost_send[0, 0], table)
    packs, merges = make_tables(tables, slots, loads.shape[0])
    partial = products(a_blocks, prolong, ghosts, neighbour)
    device = lax.axis_index("gx") * NX * NZ + lax.axis_index("gy")
    near_cols = coarse_cols - (device - 1) * loads.shape[0]
    return coarse_and_smooth(n_gx, partial, packs, merges, near_cols, loads)


def solution(mesh):
    return jax.shard_map(
        functools.partial(per_device, mesh.shape["gx"]),
        mesh=mesh,
        in_specs=(
            P(("gx", "gy"), None, None, None),
            P(("gx", "gy"), None, None),
            P(("gx", "gy"), None),
            P("gx", "gy", None, None),
            P(("gx", "gy")),
            P("gx", "gy", None),
            P(("gx", "gy"), None),
            P(("gx", "gy"), None, None),
        ),
        out_specs=(P(("gx", "gy"), None, None, None), P(("gx", "gy"), None, None)),
        check_vma=False,
    )
```

```python
import functools

import jax
import jax.numpy as jnp
from jax import lax
from jax.experimental import pallas as pl
from jax.experimental.pallas import tpu as pltpu
from jax.sharding import PartitionSpec as P

MESH = pl.DeviceIdType.MESH
NX = 4
NZ = 4
GCAP = 3
LINE = 12
SWEEPS = 2
CHUNKS = ((0, 1), (1, 2), (2, 4), (4, 6), (6, 7))
SPAN = max(k1 - k0 for k0, k1 in CHUNKS)
AHEAD = 8
TABLE = 24
VMEM = pltpu.VMEM
SMEM = pltpu.SMEM
DMA = pltpu.SemaphoreType.DMA


def place():
    me = lax.axis_index("gy")
    return lax.axis_index("gx"), lax.div(me, NZ), lax.rem(me, NZ)


def line_peer(axis, step):
    gx, x, z = place()
    if axis == 0:
        return gx, lax.rem(x + step, NX) * NZ + z
    return gx, x * NZ + lax.rem(z + step, NZ)


def greet(peers):
    barrier = pltpu.get_barrier_semaphore()
    for peer in peers:
        pl.semaphore_signal(barrier, 1, device_id=peer, device_id_type=MESH)
    pl.semaphore_wait(barrier, len(peers))


def remote(src, dst, send, recv, peer):
    return pltpu.make_async_remote_copy(
        src_ref=src, dst_ref=dst, send_sem=send, recv_sem=recv, device_id=peer, device_id_type=MESH
    )


def parts_of(width):
    cut = width // 2
    return ((0, cut), (cut, width))


def index_tables(tables, coarse_rows, coords):
    shape = (128, 128)
    lane, sub = (lax.broadcasted_iota(jnp.int32, shape, d) for d in (1, 0))
    bits = coarse_rows.bit_length() - 1

    def quarter(n):
        return sum((n >= 24 * q).astype(jnp.int32) for q in (1, 2, 3))

    def down(row):
        return jnp.transpose(jnp.broadcast_to(row, shape))

    def total(mask, values=None):
        picked = mask.astype(jnp.int32) if values is None else jnp.where(mask, values, 0)
        return jnp.sum(picked, axis=0, keepdims=True)

    lane_row = lane[0:1]
    source, source_down = quarter(lane), quarter(sub)
    source_row = source[0:1]
    packs, merges = [], []
    for axis in (0, 1):
        label = jnp.zeros((1, 128), jnp.int32)
        for s in range(4):
            entry = tables[s, coords[1], 16:24, :] if axis == 0 else tables[coords[0], s, 16:24, :]
            label += entry[axis : axis + 1]
        found = jnp.zeros((16, 128), jnp.int32)
        for owner in range(NX * NZ):
            slot_of = owner * 16 + lax.broadcasted_iota(jnp.int32, (16, 128), 0)
            found += jnp.where(slot_of == label, tables[owner // NZ, owner % NZ, 0:16, :], 0)
        target = jnp.sum(found, axis=0, keepdims=True)
        device = lax.shift_right_logical(target, bits)
        row = target & (coarse_rows - 1)
        sides = (lax.shift_right_logical(device, 2), device & 3)
        near, far = sides[axis], sides[1 - axis]
        before = sub < lane
        rank = total((down(near) == near) & (source_down == source) & before)
        used = (lane_row < 96) & (rank < LINE)
        mine = used & (near == coords[axis])
        goal = jnp.where(mine, far * coarse_rows + row, -1 - lane_row)
        order = total((down(goal) == goal) & before)
        key = down(jnp.where(mine & (order < 3), goal * 3 + order, -1))
        slot = down(source_row * LINE + rank)
        hit = key == lane
        merges.append(jnp.where(total(hit) > 0, total(hit, slot), 4 * LINE))
        own = down(jnp.where(used & (source_row == coords[axis]), near * LINE + rank, -1))
        packs.append(total(own == lane, sub - 24 * source_down))
    return jnp.concatenate(packs + merges + [jnp.zeros((4, 128), jnp.int32)])


def kernel(
    n_gx, blocks, prolong, ints, loads, coarse, smoothed,
    numbers, tables, slots_v, slots, packed, held, ghosts, arrived, partial,
    low, high, pad0, pad1, state, change, rowsum, peak, peaks,
    near_sem, block_sem, tsend1, trecv1, tsend2, trecv2, gsend1, grecv1, gsend2, grecv2, keep_sem,
    send1, recv1, send2, recv2, send3, recv3, send4, recv4, hsend, hrecv, psend, precv, *bufs,
):
    gx, x, z = place()
    gy = x * NZ + z
    coords = (x, z)
    count = NX * NZ
    fine_rows, order, width = prolong.shape
    rows = loads.shape[0]
    hrows = rows // 2
    half = order // 2
    cuts = parts_of(width)
    n_b = 2 * len(CHUNKS)
    out, pool, sums, passing, back = (bufs[n_b * n : n_b * (n + 1)] for n in range(5))
    up = (gx, lax.rem(gy + 1, count))
    down = (gx, lax.rem(gy + count - 1, count))
    across = [(lax.rem(gx + step, n_gx), gy) for step in range(1, n_gx)]
    lines = [line_peer(axis, step) for axis in (0, 1) for step in (1, 2, 3)]
    sent = []

    def go(copy):
        copy.start()
        sent.append(copy)

    def block_copy(c, i, slot):
        k0, k1 = CHUNKS[c]
        return pltpu.make_async_copy(
            blocks.at[i, pl.ds(k0, k1 - k0)], arrived.at[slot, pl.ds(0, k1 - k0)], block_sem.at[slot]
        )

    def fetch(c):
        for n in range(AHEAD):
            block_copy(c, n, n).start()

    own_numbers = pltpu.make_async_copy(ints.at[pl.ds(TABLE, numbers.shape[0])], numbers, near_sem.at[0])
    own_numbers.start()
    own_blocks = pltpu.make_async_copy(prolong, ghosts.at[pl.ds(0, fine_rows)], near_sem.at[1])
    own_blocks.start()
    table = ints.at[pl.ds(0, TABLE)]
    own_table = pltpu.make_async_copy(table, tables.at[x, z], near_sem.at[2])
    own_table.start()
    fetch(0)
    greet(lines + [up, down] + across)

    first_tables = [
        remote(table, tables.at[x, z], tsend1.at[s - 1], trecv1.at[s - 1], line_peer(0, s)) for s in (1, 2, 3)
    ]
    for copy in first_tables:
        go(copy)
    own_numbers.wait()

    for step in (2, 1, 3, 0):
        for axis in (0, 1):
            near = lax.rem(coords[axis] + step, 4)

            def pack_ghosts(n, carry, axis=axis, step=step, near=near):
                far, c = lax.div(n, GCAP), lax.rem(n, GCAP)
                peer = near * NZ + far if axis == 0 else far * NZ + near
                packed[axis, step, n] = prolong[numbers[peer, c], axis * half : (axis + 1) * half, :]
                return carry

            lax.fori_loop(0, 4 * GCAP, pack_ghosts, 0)
            if step:
                go(remote(
                    packed.at[axis, step], held.at[axis, step - 1],
                    gsend1.at[axis, step - 1], grecv1.at[axis, step - 1], line_peer(axis, step),
                ))

    own_table.wait()
    table_in = []
    for behind in (0, 1, 2, 3):
        if behind:
            first_tables[behind - 1].wait_recv()
        px = lax.rem(x + 4 - behind, 4)
        for s in (1, 2, 3):
            go(remote(
                tables.at[px, z], tables.at[px, z], tsend2.at[behind, s - 1], trecv2.at[behind, s - 1], line_peer(1, s)
            ))
            at = tables.at[px, lax.rem(z + 4 - s, 4)]
            table_in.append(remote(at, at, tsend2.at[behind, s - 1], trecv2.at[behind, s - 1], line_peer(1, s)))

    def ghost_rows(axis, px, pz):
        return ghosts.at[pl.ds(fine_rows + (px * NZ + pz) * GCAP, GCAP), pl.ds(axis * half, half), :]

    kept = []

    def forward_ghosts(behind, axis):
        if behind:
            remote(
                packed.at[axis, behind], held.at[axis, behind - 1],
                gsend1.at[axis, behind - 1], grecv1.at[axis, behind - 1], line_peer(axis, behind),
            ).wait_recv()
        at = held.at[axis, behind - 1] if behind else packed.at[axis, 0]
        near = lax.rem(coords[axis] + 4 - behind, 4)
        px, pz = (near, z) if axis == 0 else (x, near)
        for s in (1, 2, 3):
            far = lax.rem(coords[1 - axis] + s, 4)
            go(remote(
                at.at[pl.ds(far * GCAP, GCAP)], ghost_rows(axis, px, pz),
                gsend2.at[axis, behind, s - 1], grecv2.at[axis, behind, s - 1], line_peer(1 - axis, s),
            ))
        copy = pltpu.make_async_copy(
            at.at[pl.ds(coords[1 - axis] * GCAP, GCAP)], ghost_rows(axis, px, pz), keep_sem.at[axis, behind]
        )
        copy.start()
        kept.append(copy)

    def wait_ghosts():
        for axis in (0, 1):
            for behind in (0, 1, 2, 3):
                for s in (1, 2, 3):
                    near = lax.rem(coords[axis] + 4 - behind, 4)
                    far = lax.rem(coords[1 - axis] + 4 - s, 4)
                    at = ghost_rows(axis, near, far) if axis == 0 else ghost_rows(axis, far, near)
                    remote(
                        at, at, gsend2.at[axis, behind, s - 1], grecv2.at[axis, behind, s - 1], line_peer(1 - axis, s)
                    ).wait_recv()
        for copy in kept:
            copy.wait()
        own_blocks.wait()

    def multiply(c):
        k0, k1 = CHUNKS[c]

        def one_row(i, carry):
            slot = lax.rem(i, AHEAD)
            block_copy(c, i, slot).wait()
            applied = []
            for k in range(k0, k1):
                right = prolong[i] if k == 0 else ghosts[numbers[16 + i, k - 1]]
                applied.append(
                    jnp.dot(arrived[slot, k - k0], right, preferred_element_type=jnp.float32).astype(jnp.bfloat16)
                )
            value = lax.dot_general(
                prolong[i], jnp.concatenate(applied, axis=1), (((0,), (0,)), ((), ())),
                preferred_element_type=jnp.float32,
            ).astype(jnp.bfloat16)
            for k in range(k1 - k0):
                partial[i, k] = value[:, k * width : (k + 1) * width]

            @pl.when(i + AHEAD < fine_rows)
            def _():
                block_copy(c, i + AHEAD, slot).start()

            return carry

        lax.fori_loop(0, fine_rows, one_row, 0)
        if c + 1 < len(CHUNKS):
            fetch(c + 1)

    def scatter(c):
        span = CHUNKS[c][1] - CHUNKS[c][0]
        for step in (2, 1, 3, 0):
            for axis in (0, 1):
                b = 2 * c + axis
                near = lax.rem(coords[axis] + step, 4)

                def pack(n, carry, axis=axis, step=step, near=near, b=b):
                    value = partial[slots[axis, near * LINE + n], 0:span, cuts[axis][0] : cuts[axis][1], :]
                    if step:
                        out[b][step - 1, n] = value
                    else:
                        pool[b][near * LINE + n] = value
                    return carry

                lax.fori_loop(0, LINE, pack, 0)
                if step:
                    go(remote(
                        out[b].at[step - 1], pool[b].at[pl.ds(coords[axis] * LINE, LINE)],
                        send1.at[b, step - 1], recv1.at[b, step - 1], line_peer(axis, step),
                    ))
                else:
                    pool[b][4 * LINE] = jnp.zeros(pool[b].shape[1:], pool[b].dtype)

    def add_up(c):
        span = CHUNKS[c][1] - CHUNKS[c][0]
        for axis in (0, 1):
            b = 2 * c + axis
            for step in (1, 2, 3):
                source = lax.rem(coords[axis] + 4 - step, 4)
                remote(
                    out[b].at[step - 1], pool[b].at[pl.ds(source * LINE, LINE)],
                    send1.at[b, step - 1], recv1.at[b, step - 1], line_peer(axis, step),
                ).wait_recv()
            for step in (2, 1, 3, 0):
                far = lax.rem(coords[1 - axis] + step, 4)

                def merge(r, carry, axis=axis, b=b, step=step, far=far):
                    at = (far * rows + r) * 3
                    terms = [slots[2 + axis, at + n] for n in range(3)]
                    for k in range(span):
                        total = pool[b][terms[0], k].astype(jnp.float32)
                        total += pool[b][terms[1], k].astype(jnp.float32)
                        total += pool[b][terms[2], k].astype(jnp.float32)
                        sums[b][step, r, k] = total.astype(jnp.bfloat16)
                    return carry

                lax.fori_loop(0, rows, merge, 0)
                if step == 2:
                    for n, s in enumerate((1, 3)):
                        go(remote(
                            sums[b].at[2, pl.ds(n * hrows, hrows)], passing[b].at[n],
                            send2.at[b, n], recv2.at[b, n], line_peer(1 - axis, s),
                        ))
                elif step:
                    n = 0 if step == 1 else 1
                    part = pl.ds((1 - n) * hrows, hrows)
                    go(remote(
                        sums[b].at[step, part], back[b].at[n, part],
                        send3.at[b, n], recv3.at[b, n], line_peer(1 - axis, step),
                    ))

    def relay(c):
        span = CHUNKS[c][1] - CHUNKS[c][0]
        for axis in (0, 1):
            b = 2 * c + axis
            for n, step in enumerate((1, 3)):
                remote(
                    sums[b].at[2, pl.ds(n * hrows, hrows)], passing[b].at[n],
                    send2.at[b, n], recv2.at[b, n], line_peer(1 - axis, step),
                ).wait_recv()

                def take(r, carry, b=b, n=n, step=step):
                    for k in range(span):
                        total = sums[b][step, n * hrows + r, k].astype(jnp.float32)
                        total += passing[b][n, r, k].astype(jnp.float32)
                        sums[b][step, n * hrows + r, k] = total.astype(jnp.bfloat16)
                    return carry

                lax.fori_loop(0, hrows, take, 0)
                part = pl.ds(n * hrows, hrows)
                go(remote(
                    sums[b].at[step, part], back[b].at[n, part],
                    send4.at[b, n], recv4.at[b, n], line_peer(1 - axis, step),
                ))

    def finish(c):
        k0, k1 = CHUNKS[c]
        for axis in (0, 1):
            b = 2 * c + axis
            lo, hi = cuts[axis]
            for n, step in enumerate((1, 3)):
                for m, (send, recv) in enumerate(((send3, recv3), (send4, recv4))):
                    part = pl.ds((1 - n if m == 0 else n) * hrows, hrows)
                    remote(
                        sums[b].at[step, part], back[b].at[n, part],
                        send.at[b, n], recv.at[b, n], line_peer(1 - axis, step),
                    ).wait_recv()

            def settle(r, carry, b=b, lo=lo, hi=hi):
                size = jnp.zeros((hi - lo, width), jnp.float32)
                for k in range(k1 - k0):
                    total = sums[b][0, r, k].astype(jnp.float32)
                    total += back[b][0, r, k].astype(jnp.float32)
                    total += back[b][1, r, k].astype(jnp.float32)
                    rounded = total.astype(jnp.bfloat16)
                    coarse[r, k0 + k, lo:hi, :] = rounded
                    size += jnp.abs(rounded.astype(jnp.float32))
                rowsum[r, lo:hi, :] = size if c == 0 else rowsum[r, lo:hi, :] + size
                return carry

            lax.fori_loop(0, rows, settle, 0)

    multiply(0)
    for copy in table_in:
        copy.wait_recv()
    slots_v[...] = index_tables(tables, rows, coords)
    forward_ghosts(0, 0)
    forward_ghosts(0, 1)
    slot_copy = pltpu.make_async_copy(slots_v, slots, near_sem.at[3])
    slot_copy.start()
    slot_copy.wait()
    for behind in (1, 3, 2):
        for axis in (0, 1):
            forward_ghosts(behind, axis)
    scatter(0)
    wait_ghosts()
    for c in range(1, len(CHUNKS)):
        multiply(c)
        scatter(c)
        if c == 1:
            add_up(0)
        elif c == 2:
            relay(0)
    halo = [
        remote(loads, low, hsend.at[0], hrecv.at[0], up),
        remote(loads, high, hsend.at[1], hrecv.at[1], down),
    ]
    for copy in halo:
        copy.start()
    for c in range(1, len(CHUNKS)):
        add_up(c)
        if c > 1:
            relay(c - 1)
            finish(c - 2)
    relay(len(CHUNKS) - 1)
    finish(len(CHUNKS) - 2)
    finish(len(CHUNKS) - 1)

    def row_peak(r, top):
        return jnp.maximum(top, jnp.sum(rowsum[r], axis=1, keepdims=True))

    top = lax.fori_loop(0, rows, row_peak, jnp.zeros((width, 1), jnp.float32))
    peak[0] = jnp.broadcast_to(jnp.max(top, axis=0, keepdims=True), peak.shape[1:])

    base = 0
    for stage, peers in enumerate((lines[:3], lines[3:], across)):
        copies = []
        for n, peer in enumerate(peers):
            copy = remote(peak.at[stage], peaks.at[base + n], psend.at[base + n], precv.at[base + n], peer)
            copy.start()
            copies.append(copy)
        for copy in copies:
            copy.wait()
        top = peak[stage]
        for n in range(len(peers)):
            top = jnp.maximum(top, peaks[base + n])
        peak[stage + 1] = top
        base += len(peers)

    largest = peak[3, 0:1, 0:1]
    lower_end = largest / 30.0
    centre = (largest + lower_end) / 2.0
    half_width = (largest - lower_end) / 2.0
    sigma = centre / half_width
    weight = 1.0 / sigma

    def begin(r, carry):
        value = loads[r].astype(jnp.float32) / centre
        state[r] = value
        change[r] = value
        pad0[rows + r] = value.astype(jnp.bfloat16)
        return carry

    lax.fori_loop(0, rows, begin, 0)
    for copy in halo:
        copy.wait()

    def sides(r, carry):
        pad0[r] = (low[r].astype(jnp.float32) / centre).astype(jnp.bfloat16)
        pad0[2 * rows + r] = (high[r].astype(jnp.float32) / centre).astype(jnp.bfloat16)
        return carry

    lax.fori_loop(0, rows, sides, 0)

    for sweep in range(SWEEPS):
        pad = (pad0, pad1)[sweep]
        following = 1.0 / (2.0 * sigma - weight)
        keep = following * weight
        gain = 2.0 * following / half_width

        def row(r, carry, pad=pad, keep=keep, gain=gain, sweep=sweep):
            product = jnp.zeros(state.shape[1:], jnp.float32)
            for k in range(coarse.shape[1]):
                product += jnp.dot(
                    coarse[r, k], pad[numbers[40 + r, k]], preferred_element_type=jnp.float32
                )
            residual = loads[r].astype(jnp.float32) - product
            update = keep * change[r] + gain * residual
            value = state[r] + update
            if sweep + 1 < SWEEPS:
                change[r] = update
                state[r] = value
                pad1[rows + r] = value.astype(jnp.bfloat16)
            else:
                smoothed[r] = value.astype(jnp.bfloat16)
            return carry

        lax.fori_loop(0, rows, row, 0)
        weight = following
        if sweep + 1 < SWEEPS:
            own = pad1.at[pl.ds(rows, rows)]
            copies = [
                remote(own, pad1.at[pl.ds(0, rows)], hsend.at[2], hrecv.at[2], up),
                remote(own, pad1.at[pl.ds(2 * rows, rows)], hsend.at[3], hrecv.at[3], down),
            ]
            for copy in copies:
                copy.start()
            for copy in copies:
                copy.wait()
    for copy in sent:
        copy.wait_send()


def per_device(n_gx, a_blocks, prolong, neighbour, ghost_send, fine_agg, balance, coarse_cols, loads):
    fine_rows, pieces, order, _ = a_blocks.shape
    width = prolong.shape[2]
    rows, _, columns = loads.shape
    count = NX * NZ
    me = lax.axis_index("gy")
    device = lax.axis_index("gx") * count + me
    near_cols = coarse_cols - (device - 1) * rows
    lane = jnp.arange(128, dtype=jnp.int32)
    fourfold = jnp.pad(jnp.concatenate([fine_agg] * 4), (0, 128 - 4 * fine_rows))
    labels = [
        jnp.where((lane >= at * fine_rows) & (lane < (at + 1) * fine_rows), fourfold, 0)[None]
        for at in (me // NZ, me % NZ)
    ]

    def wide(values):
        return jnp.pad(values, ((0, 0), (0, 128 - values.shape[1])))

    ints = jnp.concatenate(
        [
            jnp.broadcast_to(balance[0, 0][:, None], (count, 128)),
            *labels,
            jnp.zeros((6, 128), jnp.int32),
            wide(ghost_send[0, 0]),
            wide(neighbour),
            wide(near_cols),
        ]
    )
    bf16, f32 = jnp.bfloat16, jnp.float32
    n_b = 2 * len(CHUNKS)
    peers = 6 + n_gx - 1
    shapes = [(k1 - k0, hi - lo, width) for k0, k1 in CHUNKS for lo, hi in parts_of(width)]
    bufs = [VMEM((3, LINE, *n), bf16) for n in shapes]
    bufs += [VMEM((4 * LINE + 1, *n), bf16) for n in shapes]
    bufs += [VMEM((4, rows, *n), bf16) for n in shapes]
    bufs += [VMEM((2, rows // 2, *n), bf16) for n in shapes]
    bufs += [VMEM((2, rows, *n), bf16) for n in shapes]
    vmem = pl.BlockSpec(memory_space=VMEM)
    return pl.pallas_call(
        functools.partial(kernel, n_gx),
        out_shape=(
            jax.ShapeDtypeStruct((rows, pieces, width, width), bf16),
            jax.ShapeDtypeStruct((rows, width, columns), bf16),
        ),
        in_specs=[pl.BlockSpec(memory_space=pl.ANY), vmem, vmem, vmem],
        out_specs=(vmem, vmem),
        scratch_shapes=[
            SMEM((ints.shape[0] - TABLE, 128), jnp.int32),
            VMEM((NX, NZ, TABLE, 128), jnp.int32),
            VMEM((8, 128), jnp.int32),
            SMEM((8, 128), jnp.int32),
            VMEM((2, 4, 4 * GCAP, order // 2, width), bf16),
            VMEM((2, 3, 4 * GCAP, order // 2, width), bf16),
            VMEM((fine_rows + count * GCAP, order, width), bf16),
            VMEM((AHEAD, SPAN, order, order), bf16),
            VMEM((fine_rows, SPAN, width, width), bf16),
            VMEM((rows, width, columns), bf16),
            VMEM((rows, width, columns), bf16),
            VMEM((3 * rows, width, columns), bf16),
            VMEM((3 * rows, width, columns), bf16),
            VMEM((rows, width, columns), f32),
            VMEM((rows, width, columns), f32),
            VMEM((rows, width, width), f32),
            VMEM((4, 8, 128), f32),
            VMEM((peers, 8, 128), f32),
            DMA((4,)), DMA((AHEAD,)),
            DMA((3,)), DMA((3,)), DMA((4, 3)), DMA((4, 3)),
            DMA((2, 3)), DMA((2, 3)), DMA((2, 4, 3)), DMA((2, 4, 3)), DMA((2, 4)),
            DMA((n_b, 3)), DMA((n_b, 3)),
            *[DMA((n_b, 2)) for _ in range(6)],
            DMA((4,)), DMA((4,)), DMA((peers,)), DMA((peers,)),
            *bufs,
        ],
        compiler_params=pltpu.CompilerParams(
            collective_id=1, has_side_effects=True, vmem_limit_bytes=60 << 20
        ),
        cost_estimate=pl.CostEstimate(
            flops=2 * fine_rows * pieces * order * width * (order + width),
            bytes_accessed=2 * fine_rows * pieces * order * order,
            transcendentals=0,
        ),
    )(a_blocks, prolong, ints, loads)


def solution(mesh):
    return jax.shard_map(
        functools.partial(per_device, mesh.shape["gx"]),
        mesh=mesh,
        in_specs=(
            P(("gx", "gy"), None, None, None),
            P(("gx", "gy"), None, None),
            P(("gx", "gy"), None),
            P("gx", "gy", None, None),
            P(("gx", "gy")),
            P("gx", "gy", None),
            P(("gx", "gy"), None),
            P(("gx", "gy"), None, None),
        ),
        out_specs=(P(("gx", "gy"), None, None, None), P(("gx", "gy"), None, None)),
        check_vma=False,
    )
```

```python
import functools

import jax
import jax.numpy as jnp
from jax import lax
from jax.experimental import pallas as pl
from jax.experimental.pallas import tpu as pltpu
from jax.sharding import PartitionSpec as P

MESH = pl.DeviceIdType.MESH
NX = 4
NZ = 4
GCAP = 3
LINE = 12
CHUNKS = ((0, 1), (1, 2), (2, 4), (4, 6), (6, 7))
SPAN = max(k1 - k0 for k0, k1 in CHUNKS)
AHEAD = 8
SCALE = 1.0 / 256.0
VMEM = pltpu.VMEM
SMEM = pltpu.SMEM
DMA = pltpu.SemaphoreType.DMA


def place():
    me = lax.axis_index("gy")
    return lax.axis_index("gx"), lax.div(me, NZ), lax.rem(me, NZ)


def line_peer(axis, step):
    gx, x, z = place()
    if axis == 0:
        return gx, lax.rem(x + step, NX) * NZ + z
    return gx, x * NZ + lax.rem(z + step, NZ)


def greet(peers):
    barrier = pltpu.get_barrier_semaphore()
    for peer in peers:
        pl.semaphore_signal(barrier, 1, device_id=peer, device_id_type=MESH)
    pl.semaphore_wait(barrier, len(peers))


def remote(src, dst, send, recv, peer):
    return pltpu.make_async_remote_copy(
        src_ref=src, dst_ref=dst, send_sem=send, recv_sem=recv, device_id=peer, device_id_type=MESH
    )


def parts_of(width):
    cut = width // 2
    return ((0, cut), (cut, width))


def index_tables(tables, coarse_rows, coords):
    shape = (128, 128)
    lane, sub = (lax.broadcasted_iota(jnp.int32, shape, d) for d in (1, 0))
    bits = coarse_rows.bit_length() - 1

    def quarter(n):
        return sum((n >= 24 * q).astype(jnp.int32) for q in (1, 2, 3))

    def down(row):
        return jnp.transpose(jnp.broadcast_to(row, shape))

    def total(mask, values=None):
        picked = mask.astype(jnp.int32) if values is None else jnp.where(mask, values, 0)
        return jnp.sum(picked, axis=0, keepdims=True)

    lane_row = lane[0:1]
    source, source_down = quarter(lane), quarter(sub)
    source_row = source[0:1]
    packs, merges = [], []
    for axis in (0, 1):
        label = jnp.zeros((1, 128), jnp.int32)
        for s in range(4):
            entry = tables[s, coords[1], 0:1, :] if axis == 0 else tables[coords[0], s, 0:1, :]
            label += pltpu.roll(entry, 24 * s, 1) if s else entry
        found = jnp.zeros((16, 128), jnp.int32)
        for owner in range(NX * NZ):
            slot_of = owner * 16 + lax.broadcasted_iota(jnp.int32, (16, 128), 0)
            given = down(tables[owner // NZ, owner % NZ, 1:2, :])[0:16]
            found += jnp.where(slot_of == label, given, 0)
        target = jnp.sum(found, axis=0, keepdims=True)
        device = lax.shift_right_logical(target, bits)
        row = target & (coarse_rows - 1)
        sides = (lax.shift_right_logical(device, 2), device & 3)
        near, far = sides[axis], sides[1 - axis]
        before = sub < lane
        rank = total((down(near) == near) & (source_down == source) & before)
        used = (lane_row < 96) & (rank < LINE)
        mine = used & (near == coords[axis])
        goal = jnp.where(mine, far * coarse_rows + row, -1 - lane_row)
        order = total((down(goal) == goal) & before)
        key = down(jnp.where(mine & (order < 3), goal * 3 + order, -1))
        slot = down(source_row * LINE + rank)
        hit = key == lane
        merges.append(jnp.where(total(hit) > 0, total(hit, slot), 4 * LINE))
        own = down(jnp.where(used & (source_row == coords[axis]), near * LINE + rank, -1))
        packs.append(total(own == lane, sub - 24 * source_down))
    return jnp.concatenate(packs + merges + [jnp.zeros((4, 128), jnp.int32)])


def kernel(
    n_gx, blocks, prolong, neighbours, sends, labels, balance, columns, loads, coarse, smoothed,
    near, wanted, cols, table, tables, slots_v, slots, packed, held, ghosts, arrived, partial,
    pad0, pad1, product, product_out, product_in, state, change, rowsum, peak, peaks,
    near_sem, block_sem, tsend1, trecv1, tsend2, trecv2, gsend1, grecv1, gsend2, grecv2, keep_sem,
    send1, recv1, send2, recv2, send3, recv3, send4, recv4, hsend, hrecv, psend, precv, *bufs,
):
    gx, x, z = place()
    gy = x * NZ + z
    coords = (x, z)
    count = NX * NZ
    fine_rows, order, width = prolong.shape
    rows = loads.shape[0]
    hrows = rows // 2
    half = order // 2
    cuts = parts_of(width)
    n_b = 2 * len(CHUNKS)
    out, pool, sums, passing, back = (bufs[n_b * n : n_b * (n + 1)] for n in range(5))
    up = (gx, lax.rem(gy + 1, count))
    down = (gx, lax.rem(gy + count - 1, count))
    across = [(lax.rem(gx + step, n_gx), gy) for step in range(1, n_gx)]
    lines = [line_peer(axis, step) for axis in (0, 1) for step in (1, 2, 3)]
    sent = []

    def go(copy):
        copy.start()
        sent.append(copy)

    def block_copy(c, i, slot):
        k0, k1 = CHUNKS[c]
        return pltpu.make_async_copy(
            blocks.at[i, pl.ds(k0, k1 - k0)], arrived.at[slot, pl.ds(0, k1 - k0)], block_sem.at[slot]
        )

    def fetch(c):
        for n in range(AHEAD):
            block_copy(c, n, n).start()

    own_numbers = [
        pltpu.make_async_copy(source, held_in, near_sem.at[4 + n])
        for n, (source, held_in) in enumerate(((sends, wanted), (neighbours, near), (columns, cols)))
    ]
    for copy in own_numbers:
        copy.start()
    own_blocks = pltpu.make_async_copy(prolong, ghosts.at[pl.ds(0, fine_rows)], near_sem.at[1])
    own_blocks.start()
    table[...] = jnp.zeros(table.shape, jnp.int32)
    table[0:1, 0:fine_rows] = labels[...]
    table[1:2, 0 : balance.shape[1]] = balance[...]
    own_table = pltpu.make_async_copy(table, tables.at[x, z], near_sem.at[2])
    own_table.start()
    fetch(0)

    def scale_row(r, carry):
        pad0[rows + r] = (loads[r].astype(jnp.float32) * SCALE).astype(jnp.bfloat16)
        product[r] = jnp.zeros(product.shape[1:], jnp.float32)
        return carry

    lax.fori_loop(0, rows, scale_row, 0)
    greet(lines + [up, down] + across)

    first_tables = [
        remote(table, tables.at[x, z], tsend1.at[s - 1], trecv1.at[s - 1], line_peer(0, s)) for s in (1, 2, 3)
    ]
    for copy in first_tables:
        go(copy)
    for copy in own_numbers:
        copy.wait()

    for step in (2, 1, 3, 0):
        for axis in (0, 1):
            side = lax.rem(coords[axis] + step, 4)

            def pack_ghosts(n, carry, axis=axis, step=step, side=side):
                far, c = lax.div(n, GCAP), lax.rem(n, GCAP)
                peer = side * NZ + far if axis == 0 else far * NZ + side
                packed[axis, step, n] = prolong[wanted[c, 0, peer], axis * half : (axis + 1) * half, :]
                return carry

            lax.fori_loop(0, 4 * GCAP, pack_ghosts, 0)
            if step:
                go(remote(
                    packed.at[axis, step], held.at[axis, step - 1],
                    gsend1.at[axis, step - 1], grecv1.at[axis, step - 1], line_peer(axis, step),
                ))

    own_table.wait()
    table_in = []
    for behind in (0, 1, 2, 3):
        if behind:
            first_tables[behind - 1].wait_recv()
        px = lax.rem(x + 4 - behind, 4)
        for s in (1, 2, 3):
            go(remote(
                tables.at[px, z], tables.at[px, z], tsend2.at[behind, s - 1], trecv2.at[behind, s - 1], line_peer(1, s)
            ))
            at = tables.at[px, lax.rem(z + 4 - s, 4)]
            table_in.append(remote(at, at, tsend2.at[behind, s - 1], trecv2.at[behind, s - 1], line_peer(1, s)))

    def ghost_rows(axis, px, pz):
        return ghosts.at[pl.ds(fine_rows + (px * NZ + pz) * GCAP, GCAP), pl.ds(axis * half, half), :]

    kept = []

    def forward_ghosts(behind, axis):
        if behind:
            remote(
                packed.at[axis, behind], held.at[axis, behind - 1],
                gsend1.at[axis, behind - 1], grecv1.at[axis, behind - 1], line_peer(axis, behind),
            ).wait_recv()
        at = held.at[axis, behind - 1] if behind else packed.at[axis, 0]
        side = lax.rem(coords[axis] + 4 - behind, 4)
        px, pz = (side, z) if axis == 0 else (x, side)
        for s in (1, 2, 3):
            far = lax.rem(coords[1 - axis] + s, 4)
            go(remote(
                at.at[pl.ds(far * GCAP, GCAP)], ghost_rows(axis, px, pz),
                gsend2.at[axis, behind, s - 1], grecv2.at[axis, behind, s - 1], line_peer(1 - axis, s),
            ))
        copy = pltpu.make_async_copy(
            at.at[pl.ds(coords[1 - axis] * GCAP, GCAP)], ghost_rows(axis, px, pz), keep_sem.at[axis, behind]
        )
        copy.start()
        kept.append(copy)

    def wait_ghosts():
        for axis in (0, 1):
            for behind in (0, 1, 2, 3):
                for s in (1, 2, 3):
                    side = lax.rem(coords[axis] + 4 - behind, 4)
                    far = lax.rem(coords[1 - axis] + 4 - s, 4)
                    at = ghost_rows(axis, side, far) if axis == 0 else ghost_rows(axis, far, side)
                    remote(
                        at, at, gsend2.at[axis, behind, s - 1], grecv2.at[axis, behind, s - 1], line_peer(1 - axis, s)
                    ).wait_recv()
        for copy in kept:
            copy.wait()
        own_blocks.wait()

    def multiply(c):
        k0, k1 = CHUNKS[c]

        def one_row(i, carry):
            slot = lax.rem(i, AHEAD)
            block_copy(c, i, slot).wait()
            applied = []
            for k in range(k0, k1):
                right = prolong[i] if k == 0 else ghosts[near[k - 1, i]]
                applied.append(
                    jnp.dot(arrived[slot, k - k0], right, preferred_element_type=jnp.float32).astype(jnp.bfloat16)
                )
            value = lax.dot_general(
                prolong[i], jnp.concatenate(applied, axis=1), (((0,), (0,)), ((), ())),
                preferred_element_type=jnp.float32,
            ).astype(jnp.bfloat16)
            for k in range(k1 - k0):
                partial[i, k] = value[:, k * width : (k + 1) * width]

            @pl.when(i + AHEAD < fine_rows)
            def _():
                block_copy(c, i + AHEAD, slot).start()

            return carry

        lax.fori_loop(0, fine_rows, one_row, 0)
        if c + 1 < len(CHUNKS):
            fetch(c + 1)

    def scatter(c):
        span = CHUNKS[c][1] - CHUNKS[c][0]
        for step in (2, 1, 3, 0):
            for axis in (0, 1):
                b = 2 * c + axis
                side = lax.rem(coords[axis] + step, 4)

                def pack(n, carry, axis=axis, step=step, side=side, b=b):
                    value = partial[slots[axis, side * LINE + n], 0:span, cuts[axis][0] : cuts[axis][1], :]
                    if step:
                        out[b][step - 1, n] = value
                    else:
                        pool[b][side * LINE + n] = value
                    return carry

                lax.fori_loop(0, LINE, pack, 0)
                if step:
                    go(remote(
                        out[b].at[step - 1], pool[b].at[pl.ds(coords[axis] * LINE, LINE)],
                        send1.at[b, step - 1], recv1.at[b, step - 1], line_peer(axis, step),
                    ))
                else:
                    pool[b][4 * LINE] = jnp.zeros(pool[b].shape[1:], pool[b].dtype)

    def add_up(c):
        span = CHUNKS[c][1] - CHUNKS[c][0]
        for axis in (0, 1):
            b = 2 * c + axis
            for step in (1, 2, 3):
                source = lax.rem(coords[axis] + 4 - step, 4)
                remote(
                    out[b].at[step - 1], pool[b].at[pl.ds(source * LINE, LINE)],
                    send1.at[b, step - 1], recv1.at[b, step - 1], line_peer(axis, step),
                ).wait_recv()
            for step in (2, 1, 3, 0):
                far = lax.rem(coords[1 - axis] + step, 4)

                def merge(r, carry, axis=axis, b=b, step=step, far=far):
                    at = (far * rows + r) * 3
                    terms = [slots[2 + axis, at + n] for n in range(3)]
                    for k in range(span):
                        total = pool[b][terms[0], k].astype(jnp.float32)
                        total += pool[b][terms[1], k].astype(jnp.float32)
                        total += pool[b][terms[2], k].astype(jnp.float32)
                        sums[b][step, r, k] = total.astype(jnp.bfloat16)
                    return carry

                lax.fori_loop(0, rows, merge, 0)
                if step == 2:
                    for n, s in enumerate((1, 3)):
                        go(remote(
                            sums[b].at[2, pl.ds(n * hrows, hrows)], passing[b].at[n],
                            send2.at[b, n], recv2.at[b, n], line_peer(1 - axis, s),
                        ))
                elif step:
                    n = 0 if step == 1 else 1
                    part = pl.ds((1 - n) * hrows, hrows)
                    go(remote(
                        sums[b].at[step, part], back[b].at[n, part],
                        send3.at[b, n], recv3.at[b, n], line_peer(1 - axis, step),
                    ))

    def relay(c):
        span = CHUNKS[c][1] - CHUNKS[c][0]
        for axis in (0, 1):
            b = 2 * c + axis
            for n, step in enumerate((1, 3)):
                remote(
                    sums[b].at[2, pl.ds(n * hrows, hrows)], passing[b].at[n],
                    send2.at[b, n], recv2.at[b, n], line_peer(1 - axis, step),
                ).wait_recv()

                def take(r, carry, b=b, n=n, step=step):
                    for k in range(span):
                        total = sums[b][step, n * hrows + r, k].astype(jnp.float32)
                        total += passing[b][n, r, k].astype(jnp.float32)
                        sums[b][step, n * hrows + r, k] = total.astype(jnp.bfloat16)
                    return carry

                lax.fori_loop(0, hrows, take, 0)
                part = pl.ds(n * hrows, hrows)
                go(remote(
                    sums[b].at[step, part], back[b].at[n, part],
                    send4.at[b, n], recv4.at[b, n], line_peer(1 - axis, step),
                ))

    def finish(c):
        k0, k1 = CHUNKS[c]
        for axis in (0, 1):
            b = 2 * c + axis
            lo, hi = cuts[axis]
            for n, step in enumerate((1, 3)):
                for m, (send, recv) in enumerate(((send3, recv3), (send4, recv4))):
                    part = pl.ds((1 - n if m == 0 else n) * hrows, hrows)
                    remote(
                        sums[b].at[step, part], back[b].at[n, part],
                        send.at[b, n], recv.at[b, n], line_peer(1 - axis, step),
                    ).wait_recv()

            def settle(r, carry, b=b, lo=lo, hi=hi):
                size = jnp.zeros((hi - lo, width), jnp.float32)
                for k in range(k1 - k0):
                    total = sums[b][0, r, k].astype(jnp.float32)
                    total += back[b][0, r, k].astype(jnp.float32)
                    total += back[b][1, r, k].astype(jnp.float32)
                    rounded = total.astype(jnp.bfloat16)
                    coarse[r, k0 + k, lo:hi, :] = rounded
                    size += jnp.abs(rounded.astype(jnp.float32))
                rowsum[r, lo:hi, :] = size if c == 0 else rowsum[r, lo:hi, :] + size
                return carry

            lax.fori_loop(0, rows, settle, 0)

    multiply(0)
    for copy in table_in:
        copy.wait_recv()
    slots_v[...] = index_tables(tables, rows, coords)
    forward_ghosts(0, 0)
    forward_ghosts(0, 1)
    slot_copy = pltpu.make_async_copy(slots_v, slots, near_sem.at[3])
    slot_copy.start()
    slot_copy.wait()
    for behind in (1, 3, 2):
        for axis in (0, 1):
            forward_ghosts(behind, axis)
    scatter(0)
    wait_ghosts()
    for c in range(1, len(CHUNKS)):
        multiply(c)
        scatter(c)
        if c == 1:
            add_up(0)
        elif c == 2:
            relay(0)
    own_loads = pad0.at[pl.ds(rows, rows)]
    halo = [
        remote(own_loads, pad0.at[pl.ds(0, rows)], hsend.at[0], hrecv.at[0], up),
        remote(own_loads, pad0.at[pl.ds(2 * rows, rows)], hsend.at[1], hrecv.at[1], down),
    ]
    for copy in halo:
        copy.start()
    first_col = (gx * count + gy - 1) * rows

    def padded_row(r, k):
        return jnp.clip(cols[r, k] - first_col, 0, 3 * rows - 1)

    def multiply_loads(c):
        k0, k1 = CHUNKS[c]

        def one_row(r, carry):
            total = product[r]
            for k in range(k0, k1):
                total += jnp.dot(coarse[r, k], pad0[padded_row(r, k)], preferred_element_type=jnp.float32)
            product[r] = total
            return carry

        lax.fori_loop(0, rows, one_row, 0)

    last = len(CHUNKS) - 1
    for c in range(1, last + 1):
        add_up(c)
        if c > 1:
            relay(c - 1)
            finish(c - 2)
    for copy in halo:
        copy.wait()
    for c in range(last - 1):
        multiply_loads(c)
    relay(last)
    finish(last - 1)
    multiply_loads(last - 1)
    finish(last)

    def row_peak(r, top):
        return jnp.maximum(top, jnp.sum(rowsum[r], axis=1, keepdims=True))

    top = lax.fori_loop(0, rows, row_peak, jnp.zeros((width, 1), jnp.float32))
    peak[0] = jnp.broadcast_to(jnp.max(top, axis=0, keepdims=True), peak.shape[1:])

    def ask(stage, base, peers):
        copies = [
            remote(peak.at[stage], peaks.at[base + n], psend.at[base + n], precv.at[base + n], peer)
            for n, peer in enumerate(peers)
        ]
        for copy in copies:
            copy.start()
        return copies

    def settle_peak(stage, base, copies):
        for copy in copies:
            copy.wait()
        top = peak[stage]
        for n in range(len(copies)):
            top = jnp.maximum(top, peaks[base + n])
        peak[stage + 1] = top

    asked = ask(0, 0, lines[3:])
    multiply_loads(last)

    def narrow(r, carry):
        product_out[r] = product[r].astype(jnp.bfloat16)
        return carry

    lax.fori_loop(0, rows, narrow, 0)
    halo = [
        remote(product_out, product_in.at[0], hsend.at[2], hrecv.at[2], up),
        remote(product_out, product_in.at[1], hsend.at[3], hrecv.at[3], down),
    ]
    for copy in halo:
        copy.start()
    settle_peak(0, 0, asked)
    settle_peak(1, 3, ask(1, 3, lines[:3]))
    settle_peak(2, 6, ask(2, 6, across))

    largest = peak[3, 0:1, 0:1]
    lower_end = largest / 30.0
    centre = (largest + lower_end) / 2.0
    half_width = (largest - lower_end) / 2.0
    sigma = centre / half_width
    weight = 1.0 / sigma
    following = 1.0 / (2.0 * sigma - weight)
    keep = following * weight
    gain = 2.0 * following / half_width

    def first_sweep(scaled, scaled_product):
        right = scaled.astype(jnp.float32) * (1.0 / SCALE)
        start = right / centre
        residual = right - (scaled_product.astype(jnp.float32) / centre) * (1.0 / SCALE)
        update = keep * start + gain * residual
        return start + update, update

    def own_row(r, carry):
        value, update = first_sweep(pad0[rows + r], product[r])
        state[r] = value
        change[r] = update
        pad1[rows + r] = value.astype(jnp.bfloat16)
        return carry

    lax.fori_loop(0, rows, own_row, 0)
    for n, copy in enumerate(halo):
        copy.wait()

        def side_row(r, carry, n=n):
            value, _ = first_sweep(pad0[2 * n * rows + r], product_in[n, r])
            pad1[2 * n * rows + r] = value.astype(jnp.bfloat16)
            return carry

        lax.fori_loop(0, rows, side_row, 0)

    weight = following
    following = 1.0 / (2.0 * sigma - weight)
    keep_2 = following * weight
    gain_2 = 2.0 * following / half_width

    def last_row(r, carry):
        total = jnp.zeros(state.shape[1:], jnp.float32)
        for k in range(coarse.shape[1]):
            total += jnp.dot(coarse[r, k], pad1[padded_row(r, k)], preferred_element_type=jnp.float32)
        residual = loads[r].astype(jnp.float32) - total
        smoothed[r] = (state[r] + keep_2 * change[r] + gain_2 * residual).astype(jnp.bfloat16)
        return carry

    lax.fori_loop(0, rows, last_row, 0)
    for copy in sent:
        copy.wait_send()


def per_device(n_gx, a_blocks, prolong, neighbour, ghost_send, fine_agg, balance, coarse_cols, loads):
    fine_rows, pieces, order, _ = a_blocks.shape
    width = prolong.shape[2]
    rows, _, columns = loads.shape
    count = NX * NZ
    numbers = (
        neighbour.T, ghost_send.transpose(0, 3, 1, 2)[0], fine_agg[None], balance[0, 0][None], coarse_cols
    )
    bf16, f32 = jnp.bfloat16, jnp.float32
    n_b = 2 * len(CHUNKS)
    peers = 6 + n_gx - 1
    shapes = [(k1 - k0, hi - lo, width) for k0, k1 in CHUNKS for lo, hi in parts_of(width)]
    bufs = [VMEM((3, LINE, *n), bf16) for n in shapes]
    bufs += [VMEM((4 * LINE + 1, *n), bf16) for n in shapes]
    bufs += [VMEM((4, rows, *n), bf16) for n in shapes]
    bufs += [VMEM((2, rows // 2, *n), bf16) for n in shapes]
    bufs += [VMEM((2, rows, *n), bf16) for n in shapes]
    vmem, anywhere = pl.BlockSpec(memory_space=VMEM), pl.BlockSpec(memory_space=pl.ANY)
    return pl.pallas_call(
        functools.partial(kernel, n_gx),
        out_shape=(
            jax.ShapeDtypeStruct((rows, pieces, width, width), bf16),
            jax.ShapeDtypeStruct((rows, width, columns), bf16),
        ),
        in_specs=[anywhere, vmem, anywhere, anywhere, vmem, vmem, anywhere, vmem],
        out_specs=(vmem, vmem),
        scratch_shapes=[
            SMEM((pieces - 1, fine_rows), jnp.int32),
            SMEM((GCAP, 1, count), jnp.int32),
            SMEM((rows, pieces), jnp.int32),
            VMEM((8, 128), jnp.int32),
            VMEM((NX, NZ, 8, 128), jnp.int32),
            VMEM((8, 128), jnp.int32),
            SMEM((8, 128), jnp.int32),
            VMEM((2, 4, 4 * GCAP, order // 2, width), bf16),
            VMEM((2, 3, 4 * GCAP, order // 2, width), bf16),
            VMEM((fine_rows + count * GCAP, order, width), bf16),
            VMEM((AHEAD, SPAN, order, order), bf16),
            VMEM((fine_rows, SPAN, width, width), bf16),
            VMEM((3 * rows, width, columns), bf16),
            VMEM((3 * rows, width, columns), bf16),
            VMEM((rows, width, columns), f32),
            VMEM((rows, width, columns), bf16),
            VMEM((2, rows, width, columns), bf16),
            VMEM((rows, width, columns), f32),
            VMEM((rows, width, columns), f32),
            VMEM((rows, width, width), f32),
            VMEM((4, 8, 128), f32),
            VMEM((peers, 8, 128), f32),
            DMA((8,)), DMA((AHEAD,)),
            DMA((3,)), DMA((3,)), DMA((4, 3)), DMA((4, 3)),
            DMA((2, 3)), DMA((2, 3)), DMA((2, 4, 3)), DMA((2, 4, 3)), DMA((2, 4)),
            DMA((n_b, 3)), DMA((n_b, 3)),
            *[DMA((n_b, 2)) for _ in range(6)],
            DMA((4,)), DMA((4,)), DMA((peers,)), DMA((peers,)),
            *bufs,
        ],
        compiler_params=pltpu.CompilerParams(
            collective_id=1, has_side_effects=True, vmem_limit_bytes=60 << 20
        ),
        cost_estimate=pl.CostEstimate(
            flops=2 * fine_rows * pieces * order * width * (order + width),
            bytes_accessed=2 * fine_rows * pieces * order * order,
            transcendentals=0,
        ),
    )(a_blocks, prolong, *numbers, loads)


def solution(mesh):
    return jax.shard_map(
        functools.partial(per_device, mesh.shape["gx"]),
        mesh=mesh,
        in_specs=(
            P(("gx", "gy"), None, None, None),
            P(("gx", "gy"), None, None),
            P(("gx", "gy"), None),
            P("gx", "gy", None, None),
            P(("gx", "gy")),
            P("gx", "gy", None),
            P(("gx", "gy"), None),
            P(("gx", "gy"), None, None),
        ),
        out_specs=(P(("gx", "gy"), None, None, None), P(("gx", "gy"), None, None)),
        check_vma=False,
    )
```

```python
import functools

import jax
import jax.numpy as jnp
from jax import lax
from jax.experimental import pallas as pl
from jax.experimental.pallas import tpu as pltpu
from jax.sharding import PartitionSpec as P

MESH = pl.DeviceIdType.MESH
NX = 4
NZ = 4
GCAP = 3
LINE = 12
CHUNKS = ((0, 1), (1, 2), (2, 4), (4, 6), (6, 7))
SPAN = max(k1 - k0 for k0, k1 in CHUNKS)
ROWS = 4
AHEAD = 8
SCALE = 1.0 / 256.0
VMEM = pltpu.VMEM
SMEM = pltpu.SMEM
DMA = pltpu.SemaphoreType.DMA


def place():
    me = lax.axis_index("gy")
    return lax.axis_index("gx"), lax.div(me, NZ), lax.rem(me, NZ)


def line_peer(axis, step):
    gx, x, z = place()
    if axis == 0:
        return gx, lax.rem(x + step, NX) * NZ + z
    return gx, x * NZ + lax.rem(z + step, NZ)


def greet(peers):
    barrier = pltpu.get_barrier_semaphore()
    for peer in peers:
        pl.semaphore_signal(barrier, 1, device_id=peer, device_id_type=MESH)
    pl.semaphore_wait(barrier, len(peers))


def remote(src, dst, send, recv, peer):
    return pltpu.make_async_remote_copy(
        src_ref=src, dst_ref=dst, send_sem=send, recv_sem=recv, device_id=peer, device_id_type=MESH
    )


def parts_of(width):
    cut = width // 2
    return ((0, cut), (cut, width))


def steps(count, unroll, body):
    def several(n, carry):
        for m in range(unroll):
            body(n * unroll + m)
        return carry

    lax.fori_loop(0, count // unroll, several, 0)


def index_tables(tables, coarse_rows, coords):
    shape = (128, 128)
    lane, sub = (lax.broadcasted_iota(jnp.int32, shape, d) for d in (1, 0))
    bits = coarse_rows.bit_length() - 1

    def quarter(n):
        return sum((n >= 24 * q).astype(jnp.int32) for q in (1, 2, 3))

    def down(row):
        return jnp.transpose(jnp.broadcast_to(row, shape))

    def total(mask, values=None):
        picked = mask.astype(jnp.int32) if values is None else jnp.where(mask, values, 0)
        return jnp.sum(picked, axis=0, keepdims=True)

    given = jnp.concatenate(
        [tables[owner // NZ, owner % NZ, 1:2, :] for owner in range(NX * NZ)] + [jnp.zeros((112, 128), jnp.int32)]
    )
    given = jnp.transpose(given)[0:16]
    lane_row = lane[0:1]
    source, source_down = quarter(lane), quarter(sub)
    source_row = source[0:1]
    packs, merges = [], []
    for axis in (0, 1):
        label = jnp.zeros((1, 128), jnp.int32)
        for s in range(4):
            entry = tables[s, coords[1], 0:1, :] if axis == 0 else tables[coords[0], s, 0:1, :]
            label += pltpu.roll(entry, 24 * s, 1) if s else entry
        found = jnp.zeros((16, 128), jnp.int32)
        for owner in range(NX * NZ):
            slot_of = owner * 16 + lax.broadcasted_iota(jnp.int32, (16, 128), 0)
            found += jnp.where(slot_of == label, given[:, owner : owner + 1], 0)
        target = jnp.sum(found, axis=0, keepdims=True)
        device = lax.shift_right_logical(target, bits)
        row = target & (coarse_rows - 1)
        sides = (lax.shift_right_logical(device, 2), device & 3)
        near, far = sides[axis], sides[1 - axis]
        before = sub < lane
        rank = total((down(near) == near) & (source_down == source) & before)
        used = (lane_row < 96) & (rank < LINE)
        mine = used & (near == coords[axis])
        goal = jnp.where(mine, far * coarse_rows + row, -1 - lane_row)
        order = total((down(goal) == goal) & before)
        key = down(jnp.where(mine & (order < 3), goal * 3 + order, -1))
        slot = down(source_row * LINE + rank)
        hit = key == lane
        merges.append(jnp.where(total(hit) > 0, total(hit, slot), 4 * LINE))
        own = down(jnp.where(used & (source_row == coords[axis]), near * LINE + rank, -1))
        packs.append(total(own == lane, sub - 24 * source_down))
    return jnp.concatenate(packs + merges + [jnp.zeros((4, 128), jnp.int32)])


def kernel(
    n_gx, blocks, prolong, neighbours, sends, labels, balance, columns, loads, coarse, smoothed,
    near, wanted, cols, table, tables, slots_v, slots, packed, held, ghosts, arrived, partial,
    pad0, pad1, product, product_out, product_in, state, change, rowsum, peak, peaks,
    near_sem, block_sem, tsend1, trecv1, tsend2, trecv2, gsend1, grecv1, gsend2, grecv2, keep_sem,
    send1, recv1, send2, recv2, send3, recv3, send4, recv4, hsend, hrecv, psend, precv, *bufs,
):
    gx, x, z = place()
    gy = x * NZ + z
    coords = (x, z)
    count = NX * NZ
    fine_rows, order, width = prolong.shape
    rows = loads.shape[0]
    hrows = rows // 2
    half = order // 2
    cuts = parts_of(width)
    n_b = 2 * len(CHUNKS)
    out, pool, sums, passing, back = (bufs[n_b * n : n_b * (n + 1)] for n in range(5))
    up = (gx, lax.rem(gy + 1, count))
    down = (gx, lax.rem(gy + count - 1, count))
    across = [(lax.rem(gx + step, n_gx), gy) for step in range(1, n_gx)]
    lines = [line_peer(axis, step) for axis in (0, 1) for step in (1, 2, 3)]
    sent = []

    def go(copy):
        copy.start()
        sent.append(copy)

    def block_copy(c, i, slot):
        k0, k1 = CHUNKS[c]
        return pltpu.make_async_copy(
            blocks.at[i, pl.ds(k0, k1 - k0)], arrived.at[slot, pl.ds(0, k1 - k0)], block_sem.at[slot]
        )

    def fetch(c):
        for n in range(AHEAD):
            block_copy(c, n, n).start()

    own_numbers = [
        pltpu.make_async_copy(source, held_in, near_sem.at[4 + n])
        for n, (source, held_in) in enumerate(((sends, wanted), (neighbours, near), (columns, cols)))
    ]
    for copy in own_numbers:
        copy.start()
    own_blocks = pltpu.make_async_copy(prolong, ghosts.at[pl.ds(0, fine_rows)], near_sem.at[1])
    own_blocks.start()
    table[...] = jnp.zeros(table.shape, jnp.int32)
    table[0:1, 0:fine_rows] = labels[...]
    table[1:2, 0 : balance.shape[1]] = balance[...]
    own_table = pltpu.make_async_copy(table, tables.at[x, z], near_sem.at[2])
    own_table.start()
    fetch(0)

    def scale_row(r, carry):
        pad0[rows + r] = (loads[r].astype(jnp.float32) * SCALE).astype(jnp.bfloat16)
        product[r] = jnp.zeros(product.shape[1:], jnp.float32)
        return carry

    lax.fori_loop(0, rows, scale_row, 0)
    greet(lines + [up, down] + across)

    first_tables = [
        remote(table, tables.at[x, z], tsend1.at[s - 1], trecv1.at[s - 1], line_peer(0, s)) for s in (1, 2, 3)
    ]
    for copy in first_tables:
        go(copy)
    for copy in own_numbers:
        copy.wait()

    for step in (2, 1, 3, 0):
        for axis in (0, 1):
            side = lax.rem(coords[axis] + step, 4)

            def pack_ghosts(n, axis=axis, step=step, side=side):
                far, c = lax.div(n, GCAP), lax.rem(n, GCAP)
                peer = side * NZ + far if axis == 0 else far * NZ + side
                packed[axis, step, n] = prolong[wanted[c, 0, peer], axis * half : (axis + 1) * half, :]

            steps(4 * GCAP, 6, pack_ghosts)
            if step:
                go(remote(
                    packed.at[axis, step], held.at[axis, step - 1],
                    gsend1.at[axis, step - 1], grecv1.at[axis, step - 1], line_peer(axis, step),
                ))

    own_table.wait()
    table_in = []
    for behind in (0, 1, 2, 3):
        if behind:
            first_tables[behind - 1].wait_recv()
        px = lax.rem(x + 4 - behind, 4)
        for s in (1, 2, 3):
            go(remote(
                tables.at[px, z], tables.at[px, z], tsend2.at[behind, s - 1], trecv2.at[behind, s - 1], line_peer(1, s)
            ))
            at = tables.at[px, lax.rem(z + 4 - s, 4)]
            table_in.append(remote(at, at, tsend2.at[behind, s - 1], trecv2.at[behind, s - 1], line_peer(1, s)))

    def ghost_rows(axis, px, pz):
        return ghosts.at[pl.ds(fine_rows + (px * NZ + pz) * GCAP, GCAP), pl.ds(axis * half, half), :]

    kept = []

    def forward_ghosts(behind, axis):
        if behind:
            remote(
                packed.at[axis, behind], held.at[axis, behind - 1],
                gsend1.at[axis, behind - 1], grecv1.at[axis, behind - 1], line_peer(axis, behind),
            ).wait_recv()
        at = held.at[axis, behind - 1] if behind else packed.at[axis, 0]
        side = lax.rem(coords[axis] + 4 - behind, 4)
        px, pz = (side, z) if axis == 0 else (x, side)
        for s in (1, 2, 3):
            far = lax.rem(coords[1 - axis] + s, 4)
            go(remote(
                at.at[pl.ds(far * GCAP, GCAP)], ghost_rows(axis, px, pz),
                gsend2.at[axis, behind, s - 1], grecv2.at[axis, behind, s - 1], line_peer(1 - axis, s),
            ))
        copy = pltpu.make_async_copy(
            at.at[pl.ds(coords[1 - axis] * GCAP, GCAP)], ghost_rows(axis, px, pz), keep_sem.at[axis, behind]
        )
        copy.start()
        kept.append(copy)

    def wait_ghosts():
        for axis in (0, 1):
            for behind in (0, 1, 2, 3):
                for s in (1, 2, 3):
                    side = lax.rem(coords[axis] + 4 - behind, 4)
                    far = lax.rem(coords[1 - axis] + 4 - s, 4)
                    at = ghost_rows(axis, side, far) if axis == 0 else ghost_rows(axis, far, side)
                    remote(
                        at, at, gsend2.at[axis, behind, s - 1], grecv2.at[axis, behind, s - 1], line_peer(1 - axis, s)
                    ).wait_recv()
        for copy in kept:
            copy.wait()
        own_blocks.wait()

    def multiply(c):
        k0, k1 = CHUNKS[c]

        def one_row(i):
            slot = lax.rem(i, AHEAD)
            applied = []
            for k in range(k0, k1):
                right = prolong[i] if k == 0 else ghosts[near[k - 1, i]]
                applied.append(
                    jnp.dot(arrived[slot, k - k0], right, preferred_element_type=jnp.float32).astype(jnp.bfloat16)
                )
            value = lax.dot_general(
                prolong[i], jnp.concatenate(applied, axis=1), (((0,), (0,)), ((), ())),
                preferred_element_type=jnp.float32,
            ).astype(jnp.bfloat16)
            for k in range(k1 - k0):
                partial[i, k] = value[:, k * width : (k + 1) * width]

        def some_rows(n, carry):
            first = n * ROWS
            for m in range(ROWS):
                block_copy(c, first + m, lax.rem(first + m, AHEAD)).wait()
            for m in range(ROWS):
                one_row(first + m)

            @pl.when(first + AHEAD < fine_rows)
            def _():
                for m in range(ROWS):
                    block_copy(c, first + AHEAD + m, lax.rem(first + m, AHEAD)).start()

            return carry

        lax.fori_loop(0, fine_rows // ROWS, some_rows, 0)
        if c + 1 < len(CHUNKS):
            fetch(c + 1)

    def scatter(c):
        span = CHUNKS[c][1] - CHUNKS[c][0]
        for step in (2, 1, 3, 0):
            for axis in (0, 1):
                b = 2 * c + axis
                side = lax.rem(coords[axis] + step, 4)

                def pack(n, axis=axis, step=step, side=side, b=b):
                    value = partial[slots[axis, side * LINE + n], 0:span, cuts[axis][0] : cuts[axis][1], :]
                    if step:
                        out[b][step - 1, n] = value
                    else:
                        pool[b][side * LINE + n] = value

                steps(LINE, 6, pack)
                if step:
                    go(remote(
                        out[b].at[step - 1], pool[b].at[pl.ds(coords[axis] * LINE, LINE)],
                        send1.at[b, step - 1], recv1.at[b, step - 1], line_peer(axis, step),
                    ))
                else:
                    pool[b][4 * LINE] = jnp.zeros(pool[b].shape[1:], pool[b].dtype)

    def add_up(c):
        span = CHUNKS[c][1] - CHUNKS[c][0]
        for axis in (0, 1):
            b = 2 * c + axis
            for step in (1, 2, 3):
                source = lax.rem(coords[axis] + 4 - step, 4)
                remote(
                    out[b].at[step - 1], pool[b].at[pl.ds(source * LINE, LINE)],
                    send1.at[b, step - 1], recv1.at[b, step - 1], line_peer(axis, step),
                ).wait_recv()
            for step in (2, 1, 3, 0):
                far = lax.rem(coords[1 - axis] + step, 4)

                def merge(r, axis=axis, b=b, step=step, far=far):
                    at = (far * rows + r) * 3
                    terms = [slots[2 + axis, at + n] for n in range(3)]
                    for k in range(span):
                        total = pool[b][terms[0], k].astype(jnp.float32)
                        total += pool[b][terms[1], k].astype(jnp.float32)
                        total += pool[b][terms[2], k].astype(jnp.float32)
                        sums[b][step, r, k] = total.astype(jnp.bfloat16)

                steps(rows, 4, merge)
                if step == 2:
                    for n, s in enumerate((1, 3)):
                        go(remote(
                            sums[b].at[2, pl.ds(n * hrows, hrows)], passing[b].at[n],
                            send2.at[b, n], recv2.at[b, n], line_peer(1 - axis, s),
                        ))
                elif step:
                    n = 0 if step == 1 else 1
                    part = pl.ds((1 - n) * hrows, hrows)
                    go(remote(
                        sums[b].at[step, part], back[b].at[n, part],
                        send3.at[b, n], recv3.at[b, n], line_peer(1 - axis, step),
                    ))

    def relay(c):
        span = CHUNKS[c][1] - CHUNKS[c][0]
        for axis in (0, 1):
            b = 2 * c + axis
            for n, step in enumerate((1, 3)):
                remote(
                    sums[b].at[2, pl.ds(n * hrows, hrows)], passing[b].at[n],
                    send2.at[b, n], recv2.at[b, n], line_peer(1 - axis, step),
                ).wait_recv()

                def take(r, b=b, n=n, step=step):
                    for k in range(span):
                        total = sums[b][step, n * hrows + r, k].astype(jnp.float32)
                        total += passing[b][n, r, k].astype(jnp.float32)
                        sums[b][step, n * hrows + r, k] = total.astype(jnp.bfloat16)

                steps(hrows, 4, take)
                part = pl.ds(n * hrows, hrows)
                go(remote(
                    sums[b].at[step, part], back[b].at[n, part],
                    send4.at[b, n], recv4.at[b, n], line_peer(1 - axis, step),
                ))

    def finish(c):
        k0, k1 = CHUNKS[c]
        for axis in (0, 1):
            b = 2 * c + axis
            lo, hi = cuts[axis]
            for n, step in enumerate((1, 3)):
                for m, (send, recv) in enumerate(((send3, recv3), (send4, recv4))):
                    part = pl.ds((1 - n if m == 0 else n) * hrows, hrows)
                    remote(
                        sums[b].at[step, part], back[b].at[n, part],
                        send.at[b, n], recv.at[b, n], line_peer(1 - axis, step),
                    ).wait_recv()

            def settle(r, b=b, lo=lo, hi=hi):
                size = jnp.zeros((hi - lo, width), jnp.float32)
                for k in range(k1 - k0):
                    total = sums[b][0, r, k].astype(jnp.float32)
                    total += back[b][0, r, k].astype(jnp.float32)
                    total += back[b][1, r, k].astype(jnp.float32)
                    rounded = total.astype(jnp.bfloat16)
                    coarse[r, k0 + k, lo:hi, :] = rounded
                    size += jnp.abs(rounded.astype(jnp.float32))
                rowsum[r, lo:hi, :] = size if c == 0 else rowsum[r, lo:hi, :] + size

            steps(rows, 2, settle)

    forward_ghosts(0, 0)
    forward_ghosts(0, 1)
    multiply(0)
    for copy in table_in:
        copy.wait_recv()
    slots_v[...] = index_tables(tables, rows, coords)
    slot_copy = pltpu.make_async_copy(slots_v, slots, near_sem.at[3])
    slot_copy.start()
    slot_copy.wait()
    for behind in (1, 3, 2):
        for axis in (0, 1):
            forward_ghosts(behind, axis)
    scatter(0)
    wait_ghosts()
    for c in range(1, len(CHUNKS)):
        multiply(c)
        scatter(c)
        if c == 1:
            add_up(0)
        elif c == 2:
            relay(0)
    own_loads = pad0.at[pl.ds(rows, rows)]
    halo = [
        remote(own_loads, pad0.at[pl.ds(0, rows)], hsend.at[0], hrecv.at[0], up),
        remote(own_loads, pad0.at[pl.ds(2 * rows, rows)], hsend.at[1], hrecv.at[1], down),
    ]
    for copy in halo:
        copy.start()
    first_col = (gx * count + gy - 1) * rows

    def padded_row(r, k):
        return jnp.clip(cols[r, k] - first_col, 0, 3 * rows - 1)

    def multiply_loads(c):
        k0, k1 = CHUNKS[c]

        def one_row(r):
            total = product[r]
            for k in range(k0, k1):
                total += jnp.dot(coarse[r, k], pad0[padded_row(r, k)], preferred_element_type=jnp.float32)
            product[r] = total

        steps(rows, 4, one_row)

    last = len(CHUNKS) - 1
    for c in range(1, last + 1):
        add_up(c)
        if c > 1:
            relay(c - 1)
            finish(c - 2)
    for copy in halo:
        copy.wait()
    for c in range(last - 1):
        multiply_loads(c)
    relay(last)
    finish(last - 1)
    multiply_loads(last - 1)
    finish(last)

    def row_peak(r, top):
        return jnp.maximum(top, jnp.sum(rowsum[r], axis=1, keepdims=True))

    top = lax.fori_loop(0, rows, row_peak, jnp.zeros((width, 1), jnp.float32))
    peak[0] = jnp.broadcast_to(jnp.max(top, axis=0, keepdims=True), peak.shape[1:])

    def ask(stage, base, peers):
        copies = [
            remote(peak.at[stage], peaks.at[base + n], psend.at[base + n], precv.at[base + n], peer)
            for n, peer in enumerate(peers)
        ]
        for copy in copies:
            copy.start()
        return copies

    def settle_peak(stage, base, copies):
        for copy in copies:
            copy.wait()
        top = peak[stage]
        for n in range(len(copies)):
            top = jnp.maximum(top, peaks[base + n])
        peak[stage + 1] = top

    asked = ask(0, 0, lines[3:])
    multiply_loads(last)

    def narrow(r, carry):
        product_out[r] = product[r].astype(jnp.bfloat16)
        return carry

    lax.fori_loop(0, rows, narrow, 0)
    halo = [
        remote(product_out, product_in.at[0], hsend.at[2], hrecv.at[2], up),
        remote(product_out, product_in.at[1], hsend.at[3], hrecv.at[3], down),
    ]
    for copy in halo:
        copy.start()
    settle_peak(0, 0, asked)
    settle_peak(1, 3, ask(1, 3, lines[:3]))
    settle_peak(2, 6, ask(2, 6, across))

    largest = peak[3, 0:1, 0:1]
    lower_end = largest / 30.0
    centre = (largest + lower_end) / 2.0
    half_width = (largest - lower_end) / 2.0
    sigma = centre / half_width
    weight = 1.0 / sigma
    following = 1.0 / (2.0 * sigma - weight)
    keep = following * weight
    gain = 2.0 * following / half_width

    def first_sweep(scaled, scaled_product):
        right = scaled.astype(jnp.float32) * (1.0 / SCALE)
        start = right / centre
        residual = right - (scaled_product.astype(jnp.float32) / centre) * (1.0 / SCALE)
        update = keep * start + gain * residual
        return start + update, update

    def own_row(r, carry):
        value, update = first_sweep(pad0[rows + r], product[r])
        state[r] = value
        change[r] = update
        pad1[rows + r] = value.astype(jnp.bfloat16)
        return carry

    lax.fori_loop(0, rows, own_row, 0)
    for n, copy in enumerate(halo):
        copy.wait()

        def side_row(r, carry, n=n):
            value, _ = first_sweep(pad0[2 * n * rows + r], product_in[n, r])
            pad1[2 * n * rows + r] = value.astype(jnp.bfloat16)
            return carry

        lax.fori_loop(0, rows, side_row, 0)

    weight = following
    following = 1.0 / (2.0 * sigma - weight)
    keep_2 = following * weight
    gain_2 = 2.0 * following / half_width

    def last_row(r):
        total = jnp.zeros(state.shape[1:], jnp.float32)
        for k in range(coarse.shape[1]):
            total += jnp.dot(coarse[r, k], pad1[padded_row(r, k)], preferred_element_type=jnp.float32)
        residual = loads[r].astype(jnp.float32) - total
        smoothed[r] = (state[r] + keep_2 * change[r] + gain_2 * residual).astype(jnp.bfloat16)

    steps(rows, 2, last_row)
    for copy in sent:
        copy.wait_send()


def per_device(n_gx, a_blocks, prolong, neighbour, ghost_send, fine_agg, balance, coarse_cols, loads):
    fine_rows, pieces, order, _ = a_blocks.shape
    width = prolong.shape[2]
    rows, _, columns = loads.shape
    count = NX * NZ
    numbers = (
        neighbour.T, ghost_send.transpose(0, 3, 1, 2)[0], fine_agg[None], balance[0, 0][None], coarse_cols
    )
    bf16, f32 = jnp.bfloat16, jnp.float32
    n_b = 2 * len(CHUNKS)
    peers = 6 + n_gx - 1
    shapes = [(k1 - k0, hi - lo, width) for k0, k1 in CHUNKS for lo, hi in parts_of(width)]
    bufs = [VMEM((3, LINE, *n), bf16) for n in shapes]
    bufs += [VMEM((4 * LINE + 1, *n), bf16) for n in shapes]
    bufs += [VMEM((4, rows, *n), bf16) for n in shapes]
    bufs += [VMEM((2, rows // 2, *n), bf16) for n in shapes]
    bufs += [VMEM((2, rows, *n), bf16) for n in shapes]
    vmem, anywhere = pl.BlockSpec(memory_space=VMEM), pl.BlockSpec(memory_space=pl.ANY)
    return pl.pallas_call(
        functools.partial(kernel, n_gx),
        out_shape=(
            jax.ShapeDtypeStruct((rows, pieces, width, width), bf16),
            jax.ShapeDtypeStruct((rows, width, columns), bf16),
        ),
        in_specs=[anywhere, vmem, anywhere, anywhere, vmem, vmem, anywhere, vmem],
        out_specs=(vmem, vmem),
        scratch_shapes=[
            SMEM((pieces - 1, fine_rows), jnp.int32),
            SMEM((GCAP, 1, count), jnp.int32),
            SMEM((rows, pieces), jnp.int32),
            VMEM((8, 128), jnp.int32),
            VMEM((NX, NZ, 8, 128), jnp.int32),
            VMEM((8, 128), jnp.int32),
            SMEM((8, 128), jnp.int32),
            VMEM((2, 4, 4 * GCAP, order // 2, width), bf16),
            VMEM((2, 3, 4 * GCAP, order // 2, width), bf16),
            VMEM((fine_rows + count * GCAP, order, width), bf16),
            VMEM((AHEAD, SPAN, order, order), bf16),
            VMEM((fine_rows, SPAN, width, width), bf16),
            VMEM((3 * rows, width, columns), bf16),
            VMEM((3 * rows, width, columns), bf16),
            VMEM((rows, width, columns), f32),
            VMEM((rows, width, columns), bf16),
            VMEM((2, rows, width, columns), bf16),
            VMEM((rows, width, columns), f32),
            VMEM((rows, width, columns), f32),
            VMEM((rows, width, width), f32),
            VMEM((4, 8, 128), f32),
            VMEM((peers, 8, 128), f32),
            DMA((8,)), DMA((AHEAD,)),
            DMA((3,)), DMA((3,)), DMA((4, 3)), DMA((4, 3)),
            DMA((2, 3)), DMA((2, 3)), DMA((2, 4, 3)), DMA((2, 4, 3)), DMA((2, 4)),
            DMA((n_b, 3)), DMA((n_b, 3)),
            *[DMA((n_b, 2)) for _ in range(6)],
            DMA((4,)), DMA((4,)), DMA((peers,)), DMA((peers,)),
            *bufs,
        ],
        compiler_params=pltpu.CompilerParams(
            collective_id=1, has_side_effects=True, vmem_limit_bytes=60 << 20
        ),
        cost_estimate=pl.CostEstimate(
            flops=2 * fine_rows * pieces * order * width * (order + width),
            bytes_accessed=2 * fine_rows * pieces * order * order,
            transcendentals=0,
        ),
    )(a_blocks, prolong, *numbers, loads)


def solution(mesh):
    return jax.shard_map(
        functools.partial(per_device, mesh.shape["gx"]),
        mesh=mesh,
        in_specs=(
            P(("gx", "gy"), None, None, None),
            P(("gx", "gy"), None, None),
            P(("gx", "gy"), None),
            P("gx", "gy", None, None),
            P(("gx", "gy")),
            P("gx", "gy", None),
            P(("gx", "gy"), None),
            P(("gx", "gy"), None, None),
        ),
        out_specs=(P(("gx", "gy"), None, None, None), P(("gx", "gy"), None, None)),
        check_vma=False,
    )
```

```python
import functools

import jax
import jax.numpy as jnp
from jax import lax
from jax.experimental import pallas as pl
from jax.experimental.pallas import tpu as pltpu
from jax.sharding import PartitionSpec as P

MESH = pl.DeviceIdType.MESH
NX = 4
NZ = 4
GCAP = 3
LINE = 12
CHUNKS = ((0, 1), (1, 2), (2, 4), (4, 6), (6, 7))
SPAN = max(k1 - k0 for k0, k1 in CHUNKS)
ROWS = 4
AHEAD = 8
SCALE = 1.0 / 256.0
VMEM = pltpu.VMEM
SMEM = pltpu.SMEM
DMA = pltpu.SemaphoreType.DMA


def place():
    me = lax.axis_index("gy")
    return lax.axis_index("gx"), lax.div(me, NZ), lax.rem(me, NZ)


def line_peer(axis, step):
    gx, x, z = place()
    if axis == 0:
        return gx, lax.rem(x + step, NX) * NZ + z
    return gx, x * NZ + lax.rem(z + step, NZ)


def greet(peers):
    barrier = pltpu.get_barrier_semaphore()
    for peer in peers:
        pl.semaphore_signal(barrier, 1, device_id=peer, device_id_type=MESH)


def meet(peers):
    pl.semaphore_wait(pltpu.get_barrier_semaphore(), len(peers))


def remote(src, dst, send, recv, peer):
    return pltpu.make_async_remote_copy(
        src_ref=src, dst_ref=dst, send_sem=send, recv_sem=recv, device_id=peer, device_id_type=MESH
    )


def parts_of(width):
    cut = width // 2
    return ((0, cut), (cut, width))


def steps(count, unroll, body):
    def several(n, carry):
        for m in range(unroll):
            body(n * unroll + m)
        return carry

    lax.fori_loop(0, count // unroll, several, 0)


def index_tables(tables, coarse_rows, coords):
    shape = (128, 128)
    lane, sub = (lax.broadcasted_iota(jnp.int32, shape, d) for d in (1, 0))
    bits = coarse_rows.bit_length() - 1

    def quarter(n):
        return sum((n >= 24 * q).astype(jnp.int32) for q in (1, 2, 3))

    def down(row):
        return jnp.transpose(jnp.broadcast_to(row, shape))

    def total(mask, values=None):
        picked = mask.astype(jnp.int32) if values is None else jnp.where(mask, values, 0)
        return jnp.sum(picked, axis=0, keepdims=True)

    given = jnp.concatenate(
        [tables[owner // NZ, owner % NZ, 1:2, :] for owner in range(NX * NZ)] + [jnp.zeros((112, 128), jnp.int32)]
    )
    given = jnp.transpose(given)[0:16]
    lane_row = lane[0:1]
    source, source_down = quarter(lane), quarter(sub)
    source_row = source[0:1]
    packs, merges = [], []
    for axis in (0, 1):
        label = jnp.zeros((1, 128), jnp.int32)
        for s in range(4):
            entry = tables[s, coords[1], 0:1, :] if axis == 0 else tables[coords[0], s, 0:1, :]
            label += pltpu.roll(entry, 24 * s, 1) if s else entry
        found = jnp.zeros((16, 128), jnp.int32)
        for owner in range(NX * NZ):
            slot_of = owner * 16 + lax.broadcasted_iota(jnp.int32, (16, 128), 0)
            found += jnp.where(slot_of == label, given[:, owner : owner + 1], 0)
        target = jnp.sum(found, axis=0, keepdims=True)
        device = lax.shift_right_logical(target, bits)
        row = target & (coarse_rows - 1)
        sides = (lax.shift_right_logical(device, 2), device & 3)
        near, far = sides[axis], sides[1 - axis]
        before = sub < lane
        rank = total((down(near) == near) & (source_down == source) & before)
        used = (lane_row < 96) & (rank < LINE)
        mine = used & (near == coords[axis])
        goal = jnp.where(mine, far * coarse_rows + row, -1 - lane_row)
        order = total((down(goal) == goal) & before)
        key = down(jnp.where(mine & (order < 3), goal * 3 + order, -1))
        slot = down(source_row * LINE + rank)
        hit = key == lane
        merges.append(jnp.where(total(hit) > 0, total(hit, slot), 4 * LINE))
        own = down(jnp.where(used & (source_row == coords[axis]), near * LINE + rank, -1))
        packs.append(total(own == lane, sub - 24 * source_down))
    return jnp.concatenate(packs + merges + [jnp.zeros((4, 128), jnp.int32)])


def kernel(
    n_gx, blocks, prolong, neighbours, sends, labels, balance, columns, loads, coarse, smoothed,
    near, wanted, cols, table, tables, slots_v, slots, packed, held, ghosts, arrived, partial,
    pad0, pad1, product, product_out, product_in, state, change, rowsum, peak, peaks,
    near_sem, block_sem, tsend1, trecv1, tsend2, trecv2, gsend1, grecv1, gsend2, grecv2, keep_sem,
    send1, recv1, send2, recv2, send3, recv3, send4, recv4, hsend, hrecv, psend, precv, *bufs,
):
    gx, x, z = place()
    gy = x * NZ + z
    coords = (x, z)
    count = NX * NZ
    fine_rows, order, width = prolong.shape
    rows = loads.shape[0]
    hrows = rows // 2
    half = order // 2
    cuts = parts_of(width)
    n_b = 2 * len(CHUNKS)
    out, pool, sums, passing, back = (bufs[n_b * n : n_b * (n + 1)] for n in range(5))
    up = (gx, lax.rem(gy + 1, count))
    down = (gx, lax.rem(gy + count - 1, count))
    across = [(lax.rem(gx + step, n_gx), gy) for step in range(1, n_gx)]
    lines = [line_peer(axis, step) for axis in (0, 1) for step in (1, 2, 3)]
    sent = []

    def go(copy):
        copy.start()
        sent.append(copy)

    def block_copy(c, i, slot):
        k0, k1 = CHUNKS[c]
        return pltpu.make_async_copy(
            blocks.at[i, pl.ds(k0, k1 - k0)], arrived.at[slot, pl.ds(0, k1 - k0)], block_sem.at[slot]
        )

    def fetch(c):
        for n in range(AHEAD):
            block_copy(c, n, n).start()

    greet(lines + [up, down] + across)
    own_numbers = [
        pltpu.make_async_copy(source, held_in, near_sem.at[4 + n])
        for n, (source, held_in) in enumerate(((sends, wanted), (neighbours, near), (columns, cols)))
    ]
    for copy in own_numbers:
        copy.start()
    own_blocks = pltpu.make_async_copy(prolong, ghosts.at[pl.ds(0, fine_rows)], near_sem.at[1])
    own_blocks.start()
    table[...] = jnp.zeros(table.shape, jnp.int32)
    table[0:1, 0:fine_rows] = labels[...]
    table[1:2, 0 : balance.shape[1]] = balance[...]
    own_table = pltpu.make_async_copy(table, tables.at[x, z], near_sem.at[2])
    own_table.start()
    fetch(0)
    for copy in own_numbers:
        copy.wait()

    for step in (2, 1, 3, 0):
        for axis in (0, 1):
            side = lax.rem(coords[axis] + step, 4)

            def pack_ghosts(n, axis=axis, step=step, side=side):
                far, c = lax.div(n, GCAP), lax.rem(n, GCAP)
                peer = side * NZ + far if axis == 0 else far * NZ + side
                packed[axis, step, n] = prolong[wanted[c, 0, peer], axis * half : (axis + 1) * half, :]

            steps(4 * GCAP, 6, pack_ghosts)

    meet(lines + [up, down] + across)

    first_tables = [
        remote(table, tables.at[x, z], tsend1.at[s - 1], trecv1.at[s - 1], line_peer(0, s)) for s in (1, 2, 3)
    ]
    for copy in first_tables:
        go(copy)
    for step in (2, 1, 3):
        for axis in (0, 1):
            go(remote(
                packed.at[axis, step], held.at[axis, step - 1],
                gsend1.at[axis, step - 1], grecv1.at[axis, step - 1], line_peer(axis, step),
            ))

    own_table.wait()
    table_in = []
    for behind in (0, 1, 2, 3):
        if behind:
            first_tables[behind - 1].wait_recv()
        px = lax.rem(x + 4 - behind, 4)
        for s in (1, 2, 3):
            go(remote(
                tables.at[px, z], tables.at[px, z], tsend2.at[behind, s - 1], trecv2.at[behind, s - 1], line_peer(1, s)
            ))
            at = tables.at[px, lax.rem(z + 4 - s, 4)]
            table_in.append(remote(at, at, tsend2.at[behind, s - 1], trecv2.at[behind, s - 1], line_peer(1, s)))

    def ghost_rows(axis, px, pz):
        return ghosts.at[pl.ds(fine_rows + (px * NZ + pz) * GCAP, GCAP), pl.ds(axis * half, half), :]

    kept = []

    def forward_ghosts(behind, axis):
        if behind:
            remote(
                packed.at[axis, behind], held.at[axis, behind - 1],
                gsend1.at[axis, behind - 1], grecv1.at[axis, behind - 1], line_peer(axis, behind),
            ).wait_recv()
        at = held.at[axis, behind - 1] if behind else packed.at[axis, 0]
        side = lax.rem(coords[axis] + 4 - behind, 4)
        px, pz = (side, z) if axis == 0 else (x, side)
        for s in (1, 2, 3):
            far = lax.rem(coords[1 - axis] + s, 4)
            go(remote(
                at.at[pl.ds(far * GCAP, GCAP)], ghost_rows(axis, px, pz),
                gsend2.at[axis, behind, s - 1], grecv2.at[axis, behind, s - 1], line_peer(1 - axis, s),
            ))
        copy = pltpu.make_async_copy(
            at.at[pl.ds(coords[1 - axis] * GCAP, GCAP)], ghost_rows(axis, px, pz), keep_sem.at[axis, behind]
        )
        copy.start()
        kept.append(copy)

    def wait_ghosts():
        for axis in (0, 1):
            for behind in (0, 1, 2, 3):
                for s in (1, 2, 3):
                    side = lax.rem(coords[axis] + 4 - behind, 4)
                    far = lax.rem(coords[1 - axis] + 4 - s, 4)
                    at = ghost_rows(axis, side, far) if axis == 0 else ghost_rows(axis, far, side)
                    remote(
                        at, at, gsend2.at[axis, behind, s - 1], grecv2.at[axis, behind, s - 1], line_peer(1 - axis, s)
                    ).wait_recv()
        for copy in kept:
            copy.wait()
        own_blocks.wait()

    def multiply(c):
        k0, k1 = CHUNKS[c]

        def one_row(i):
            slot = lax.rem(i, AHEAD)
            applied = []
            for k in range(k0, k1):
                right = prolong[i] if k == 0 else ghosts[near[k - 1, i]]
                applied.append(
                    jnp.dot(arrived[slot, k - k0], right, preferred_element_type=jnp.float32).astype(jnp.bfloat16)
                )
            value = lax.dot_general(
                prolong[i], jnp.concatenate(applied, axis=1), (((0,), (0,)), ((), ())),
                preferred_element_type=jnp.float32,
            ).astype(jnp.bfloat16)
            for k in range(k1 - k0):
                partial[i, k] = value[:, k * width : (k + 1) * width]

        def some_rows(n, carry):
            first = n * ROWS
            for m in range(ROWS):
                block_copy(c, first + m, lax.rem(first + m, AHEAD)).wait()
            for m in range(ROWS):
                one_row(first + m)

            @pl.when(first + AHEAD < fine_rows)
            def _():
                for m in range(ROWS):
                    block_copy(c, first + AHEAD + m, lax.rem(first + m, AHEAD)).start()

            return carry

        lax.fori_loop(0, fine_rows // ROWS, some_rows, 0)
        if c + 1 < len(CHUNKS):
            fetch(c + 1)

    def scatter(c):
        span = CHUNKS[c][1] - CHUNKS[c][0]
        for step in (2, 1, 3, 0):
            for axis in (0, 1):
                b = 2 * c + axis
                side = lax.rem(coords[axis] + step, 4)

                def pack(n, axis=axis, step=step, side=side, b=b):
                    value = partial[slots[axis, side * LINE + n], 0:span, cuts[axis][0] : cuts[axis][1], :]
                    if step:
                        out[b][step - 1, n] = value
                    else:
                        pool[b][side * LINE + n] = value

                steps(LINE, 6, pack)
                if step:
                    go(remote(
                        out[b].at[step - 1], pool[b].at[pl.ds(coords[axis] * LINE, LINE)],
                        send1.at[b, step - 1], recv1.at[b, step - 1], line_peer(axis, step),
                    ))
                else:
                    pool[b][4 * LINE] = jnp.zeros(pool[b].shape[1:], pool[b].dtype)

    def add_up(c):
        span = CHUNKS[c][1] - CHUNKS[c][0]
        for axis in (0, 1):
            b = 2 * c + axis
            for step in (1, 2, 3):
                source = lax.rem(coords[axis] + 4 - step, 4)
                remote(
                    out[b].at[step - 1], pool[b].at[pl.ds(source * LINE, LINE)],
                    send1.at[b, step - 1], recv1.at[b, step - 1], line_peer(axis, step),
                ).wait_recv()
            for step in (2, 1, 3, 0):
                far = lax.rem(coords[1 - axis] + step, 4)

                def merge(r, axis=axis, b=b, step=step, far=far):
                    at = (far * rows + r) * 3
                    terms = [slots[2 + axis, at + n] for n in range(3)]
                    for k in range(span):
                        total = pool[b][terms[0], k].astype(jnp.float32)
                        total += pool[b][terms[1], k].astype(jnp.float32)
                        total += pool[b][terms[2], k].astype(jnp.float32)
                        sums[b][step, r, k] = total.astype(jnp.bfloat16)

                steps(rows, 4, merge)
                if step == 2:
                    for n, s in enumerate((1, 3)):
                        go(remote(
                            sums[b].at[2, pl.ds(n * hrows, hrows)], passing[b].at[n],
                            send2.at[b, n], recv2.at[b, n], line_peer(1 - axis, s),
                        ))
                elif step:
                    n = 0 if step == 1 else 1
                    part = pl.ds((1 - n) * hrows, hrows)
                    go(remote(
                        sums[b].at[step, part], back[b].at[n, part],
                        send3.at[b, n], recv3.at[b, n], line_peer(1 - axis, step),
                    ))

    def relay(c):
        span = CHUNKS[c][1] - CHUNKS[c][0]
        for axis in (0, 1):
            b = 2 * c + axis
            for n, step in enumerate((1, 3)):
                remote(
                    sums[b].at[2, pl.ds(n * hrows, hrows)], passing[b].at[n],
                    send2.at[b, n], recv2.at[b, n], line_peer(1 - axis, step),
                ).wait_recv()

                def take(r, b=b, n=n, step=step):
                    for k in range(span):
                        total = sums[b][step, n * hrows + r, k].astype(jnp.float32)
                        total += passing[b][n, r, k].astype(jnp.float32)
                        sums[b][step, n * hrows + r, k] = total.astype(jnp.bfloat16)

                steps(hrows, 4, take)
                part = pl.ds(n * hrows, hrows)
                go(remote(
                    sums[b].at[step, part], back[b].at[n, part],
                    send4.at[b, n], recv4.at[b, n], line_peer(1 - axis, step),
                ))

    def finish(c):
        k0, k1 = CHUNKS[c]
        for axis in (0, 1):
            b = 2 * c + axis
            lo, hi = cuts[axis]
            for n, step in enumerate((1, 3)):
                for m, (send, recv) in enumerate(((send3, recv3), (send4, recv4))):
                    part = pl.ds((1 - n if m == 0 else n) * hrows, hrows)
                    remote(
                        sums[b].at[step, part], back[b].at[n, part],
                        send.at[b, n], recv.at[b, n], line_peer(1 - axis, step),
                    ).wait_recv()

            def settle(r, b=b, lo=lo, hi=hi):
                size = jnp.zeros((hi - lo, width), jnp.float32)
                for k in range(k1 - k0):
                    total = sums[b][0, r, k].astype(jnp.float32)
                    total += back[b][0, r, k].astype(jnp.float32)
                    total += back[b][1, r, k].astype(jnp.float32)
                    rounded = total.astype(jnp.bfloat16)
                    coarse[r, k0 + k, lo:hi, :] = rounded
                    size += jnp.abs(rounded.astype(jnp.float32))
                rowsum[r, lo:hi, :] = size if c == 0 else rowsum[r, lo:hi, :] + size

            steps(rows, 2, settle)

    forward_ghosts(0, 0)
    forward_ghosts(0, 1)
    def scale_row(r, carry):
        pad0[rows + r] = (loads[r].astype(jnp.float32) * SCALE).astype(jnp.bfloat16)
        product[r] = jnp.zeros(product.shape[1:], jnp.float32)
        return carry

    lax.fori_loop(0, rows, scale_row, 0)
    multiply(0)
    for behind in (1, 3, 2):
        for axis in (0, 1):
            forward_ghosts(behind, axis)
    for copy in table_in:
        copy.wait_recv()
    slots_v[...] = index_tables(tables, rows, coords)
    slot_copy = pltpu.make_async_copy(slots_v, slots, near_sem.at[3])
    slot_copy.start()
    slot_copy.wait()
    scatter(0)
    wait_ghosts()
    for c in range(1, len(CHUNKS)):
        multiply(c)
        scatter(c)
        if c == 1:
            add_up(0)
        elif c == 2:
            relay(0)
    own_loads = pad0.at[pl.ds(rows, rows)]
    halo = [
        remote(own_loads, pad0.at[pl.ds(0, rows)], hsend.at[0], hrecv.at[0], up),
        remote(own_loads, pad0.at[pl.ds(2 * rows, rows)], hsend.at[1], hrecv.at[1], down),
    ]
    for copy in halo:
        copy.start()
    first_col = (gx * count + gy - 1) * rows

    def padded_row(r, k):
        return jnp.clip(cols[r, k] - first_col, 0, 3 * rows - 1)

    def multiply_loads(c):
        k0, k1 = CHUNKS[c]

        def one_row(r):
            total = product[r]
            for k in range(k0, k1):
                total += jnp.dot(coarse[r, k], pad0[padded_row(r, k)], preferred_element_type=jnp.float32)
            product[r] = total

        steps(rows, 4, one_row)

    last = len(CHUNKS) - 1
    for c in range(1, last + 1):
        add_up(c)
        if c > 1:
            relay(c - 1)
            finish(c - 2)
    for copy in halo:
        copy.wait()
    for c in range(last - 1):
        multiply_loads(c)
    relay(last)
    finish(last - 1)
    multiply_loads(last - 1)
    finish(last)

    def row_peak(r, top):
        return jnp.maximum(top, jnp.sum(rowsum[r], axis=1, keepdims=True))

    top = lax.fori_loop(0, rows, row_peak, jnp.zeros((width, 1), jnp.float32))
    peak[0] = jnp.broadcast_to(jnp.max(top, axis=0, keepdims=True), peak.shape[1:])

    def ask(stage, base, peers):
        copies = [
            remote(peak.at[stage], peaks.at[base + n], psend.at[base + n], precv.at[base + n], peer)
            for n, peer in enumerate(peers)
        ]
        for copy in copies:
            copy.start()
        return copies

    def settle_peak(stage, base, copies):
        for copy in copies:
            copy.wait()
        top = peak[stage]
        for n in range(len(copies)):
            top = jnp.maximum(top, peaks[base + n])
        peak[stage + 1] = top

    asked = ask(0, 0, lines[3:])
    multiply_loads(last)

    def narrow(r, carry):
        product_out[r] = product[r].astype(jnp.bfloat16)
        return carry

    lax.fori_loop(0, rows, narrow, 0)
    halo = [
        remote(product_out, product_in.at[0], hsend.at[2], hrecv.at[2], up),
        remote(product_out, product_in.at[1], hsend.at[3], hrecv.at[3], down),
    ]
    for copy in halo:
        copy.start()
    settle_peak(0, 0, asked)
    settle_peak(1, 3, ask(1, 3, lines[:3]))
    settle_peak(2, 6, ask(2, 6, across))

    largest = peak[3, 0:1, 0:1]
    lower_end = largest / 30.0
    centre = (largest + lower_end) / 2.0
    half_width = (largest - lower_end) / 2.0
    sigma = centre / half_width
    weight = 1.0 / sigma
    following = 1.0 / (2.0 * sigma - weight)
    keep = following * weight
    gain = 2.0 * following / half_width

    def first_sweep(scaled, scaled_product):
        right = scaled.astype(jnp.float32) * (1.0 / SCALE)
        start = right / centre
        residual = right - (scaled_product.astype(jnp.float32) / centre) * (1.0 / SCALE)
        update = keep * start + gain * residual
        return start + update, update

    def own_row(r, carry):
        value, update = first_sweep(pad0[rows + r], product[r])
        state[r] = value
        change[r] = update
        pad1[rows + r] = value.astype(jnp.bfloat16)
        return carry

    lax.fori_loop(0, rows, own_row, 0)
    for n, copy in enumerate(halo):
        copy.wait()

        def side_row(r, carry, n=n):
            value, _ = first_sweep(pad0[2 * n * rows + r], product_in[n, r])
            pad1[2 * n * rows + r] = value.astype(jnp.bfloat16)
            return carry

        lax.fori_loop(0, rows, side_row, 0)

    weight = following
    following = 1.0 / (2.0 * sigma - weight)
    keep_2 = following * weight
    gain_2 = 2.0 * following / half_width

    def last_row(r):
        total = jnp.zeros(state.shape[1:], jnp.float32)
        for k in range(coarse.shape[1]):
            total += jnp.dot(coarse[r, k], pad1[padded_row(r, k)], preferred_element_type=jnp.float32)
        residual = loads[r].astype(jnp.float32) - total
        smoothed[r] = (state[r] + keep_2 * change[r] + gain_2 * residual).astype(jnp.bfloat16)

    steps(rows, 2, last_row)
    for copy in sent:
        copy.wait_send()


def per_device(n_gx, a_blocks, prolong, neighbour, ghost_send, fine_agg, balance, coarse_cols, loads):
    fine_rows, pieces, order, _ = a_blocks.shape
    width = prolong.shape[2]
    rows, _, columns = loads.shape
    count = NX * NZ
    numbers = (
        neighbour.T, ghost_send.transpose(0, 3, 1, 2)[0], fine_agg[None], balance[0, 0][None], coarse_cols
    )
    bf16, f32 = jnp.bfloat16, jnp.float32
    n_b = 2 * len(CHUNKS)
    peers = 6 + n_gx - 1
    shapes = [(k1 - k0, hi - lo, width) for k0, k1 in CHUNKS for lo, hi in parts_of(width)]
    bufs = [VMEM((3, LINE, *n), bf16) for n in shapes]
    bufs += [VMEM((4 * LINE + 1, *n), bf16) for n in shapes]
    bufs += [VMEM((4, rows, *n), bf16) for n in shapes]
    bufs += [VMEM((2, rows // 2, *n), bf16) for n in shapes]
    bufs += [VMEM((2, rows, *n), bf16) for n in shapes]
    vmem, anywhere = pl.BlockSpec(memory_space=VMEM), pl.BlockSpec(memory_space=pl.ANY)
    return pl.pallas_call(
        functools.partial(kernel, n_gx),
        out_shape=(
            jax.ShapeDtypeStruct((rows, pieces, width, width), bf16),
            jax.ShapeDtypeStruct((rows, width, columns), bf16),
        ),
        in_specs=[anywhere, vmem, anywhere, anywhere, vmem, vmem, anywhere, vmem],
        out_specs=(vmem, vmem),
        scratch_shapes=[
            SMEM((pieces - 1, fine_rows), jnp.int32),
            SMEM((GCAP, 1, count), jnp.int32),
            SMEM((rows, pieces), jnp.int32),
            VMEM((8, 128), jnp.int32),
            VMEM((NX, NZ, 8, 128), jnp.int32),
            VMEM((8, 128), jnp.int32),
            SMEM((8, 128), jnp.int32),
            VMEM((2, 4, 4 * GCAP, order // 2, width), bf16),
            VMEM((2, 3, 4 * GCAP, order // 2, width), bf16),
            VMEM((fine_rows + count * GCAP, order, width), bf16),
            VMEM((AHEAD, SPAN, order, order), bf16),
            VMEM((fine_rows, SPAN, width, width), bf16),
            VMEM((3 * rows, width, columns), bf16),
            VMEM((3 * rows, width, columns), bf16),
            VMEM((rows, width, columns), f32),
            VMEM((rows, width, columns), bf16),
            VMEM((2, rows, width, columns), bf16),
            VMEM((rows, width, columns), f32),
            VMEM((rows, width, columns), f32),
            VMEM((rows, width, width), f32),
            VMEM((4, 8, 128), f32),
            VMEM((peers, 8, 128), f32),
            DMA((8,)), DMA((AHEAD,)),
            DMA((3,)), DMA((3,)), DMA((4, 3)), DMA((4, 3)),
            DMA((2, 3)), DMA((2, 3)), DMA((2, 4, 3)), DMA((2, 4, 3)), DMA((2, 4)),
            DMA((n_b, 3)), DMA((n_b, 3)),
            *[DMA((n_b, 2)) for _ in range(6)],
            DMA((4,)), DMA((4,)), DMA((peers,)), DMA((peers,)),
            *bufs,
        ],
        compiler_params=pltpu.CompilerParams(
            collective_id=1, has_side_effects=True, vmem_limit_bytes=60 << 20
        ),
        cost_estimate=pl.CostEstimate(
            flops=2 * fine_rows * pieces * order * width * (order + width),
            bytes_accessed=2 * fine_rows * pieces * order * order,
            transcendentals=0,
        ),
    )(a_blocks, prolong, *numbers, loads)


def solution(mesh):
    return jax.shard_map(
        functools.partial(per_device, mesh.shape["gx"]),
        mesh=mesh,
        in_specs=(
            P(("gx", "gy"), None, None, None),
            P(("gx", "gy"), None, None),
            P(("gx", "gy"), None),
            P("gx", "gy", None, None),
            P(("gx", "gy")),
            P("gx", "gy", None),
            P(("gx", "gy"), None),
            P(("gx", "gy"), None, None),
        ),
        out_specs=(P(("gx", "gy"), None, None, None), P(("gx", "gy"), None, None)),
        check_vma=False,
    )
```
